1024 devices in a mesh: dp: 4 (over x), expert: 32 (over y, z_lo), tensor: 8 (over z_hi, core).
Axes of the slice: x: 4, y: 4, z: 32 (z_hi: 4, z_lo: 8; z = z_hi * 8 + z_lo), core: 2. Of those that a mesh axis runs over, the one named last changes fastest.
Arguments:
- hidden_states: bfloat16 [8192, 2048], P(('dp', 'expert'), 'tensor'), may hold values from -6 to 6
- expert_ids: int32 [8192, 8], P(('dp', 'expert')), may hold values from 0 to 63, all different within a row; in each aligned block of 64 rows (0 to 63, 64 to 127, ...) at most 8 rows name the same one
- gate_weights: bfloat16 [8192, 8], P(('dp', 'expert')), may hold values from 0.029907227 to 0.3984375
- completion_lengths: int32 [4], P('dp'), may hold values from 256 to 2048
- output_grad: bfloat16 [8192, 2048], P(('dp', 'expert'), 'tensor'), may hold values from -3 to 3
- gate_up_proj: bfloat16 [64, 2, 1536, 2048], P('expert', None, 'tensor'), may hold values from -0.125 to 0.125
- down_proj: bfloat16 [64, 1536, 2048], P('expert', 'tensor'), may hold values from -0.15625 to 0.15625
Outputs:
- input_grad: bfloat16 [8192, 2048], P(('dp', 'expert'), 'tensor')
- gate_grad: float32 [8192, 8], P(('dp', 'expert'), 'tensor')
- gate_up_grad: bfloat16 [64, 2, 1536, 2048], P('expert', None, 'tensor', 'dp')
- down_grad: bfloat16 [64, 1536, 2048], P('expert', 'tensor', 'dp')
The draws below stay inside these ranges and needn't reach their ends.
Inputs may be any that keep to these rules, and one draw needn't show every extreme that they name: `expert_ids`: among the routes of the 64 tokens of one index of dp and expert together, every expert is named exactly 8 times.
All inputs are finite; a program needn't handle non-finite values.
Results may differ from the reference program's by a relative error of at most 0.028.
Values may be sent and summed in bfloat16 or wider, within the bound.
No kernel may reach another device: no remote copies, remote signals or barrier semaphores. Data moves between devices by JAX's collectives and lax.ppermute only.
A program may use at most 64 MiB of HBM per device.

```python
import math
import jax
import jax.numpy as jnp
import numpy as np
from jax import lax

D = 2048
FF = 1536
FFB = 192
EXPERTS = 64
TOP = 8
TOK_G = 64
CAP = 8
SEQ = 2048
COMPLETIONS = 4
TOKENS = 8192
N_EXPERT = 32
N_TENSOR = 8


def touch_ends(array, stream_key, low, high):
    place = [jax.random.randint(jax.random.fold_in(stream_key, axis), (), 0, length) for axis, length in enumerate(array.shape)]
    widest = array.shape.index(max(array.shape))
    neighbour = place[:widest] + [(place[widest] + 1) % array.shape[widest]] + place[widest + 1:]
    return array.at[tuple(place)].set(low).at[tuple(neighbour)].set(high)


def block_scale(rng, shape, pieces, smallest, largest):
    level, own = 1.0, jax.random.fold_in(rng, 6)
    for dim, shards_of in pieces:
        steps = jnp.exp(jax.random.uniform(jax.random.fold_in(own, dim), (shards_of,), jnp.float32, smallest / len(pieces), largest / len(pieces)))
        level = level * jnp.repeat(steps, shape[dim] // shards_of).reshape([-1 if axis == dim else 1 for axis in range(len(shape))])
    return level


def assign_block(key, own, number, rows, count, top, bound, lean):
    sequence = jax.random.permutation(key, count)
    packed, ordinary = load_shares(count, rows * top, bound, lean, True), load_shares(count, rows * top, bound, lean, False)
    places = jnp.arange(count)

    def named(sizes, offset_by):
        used = int((sizes > 0).sum())
        fixed = max(1, used // 4)
        moved = fixed + (places - fixed + offset_by * (used - fixed)) % max(1, count - fixed)
        return jnp.zeros((count,), jnp.int32).at[sequence[jnp.where(places < fixed, places, moved)]].set(jnp.asarray(sizes, jnp.int32))

    sizes = jnp.where(number % 4 == 0, named(packed, number // 4), named(ordinary, number - number // 4 - 1))
    mixed = jax.random.permutation(jax.random.fold_in(own, 3), count)
    source_of, receiver = mixed[0:count // 2 * 2:2], mixed[1:count // 2 * 2:2]
    room = jnp.minimum(sizes[source_of] - 1, bound - sizes[receiver]) // 2
    room = jnp.where((source_of == sequence[0]) | (receiver == sequence[0]) | (sizes[receiver] == 0), 0, jnp.maximum(room, 0))
    moved = jax.random.randint(jax.random.fold_in(own, 4), (count // 2,), 0, 1 << 20) % (room + 1)
    sizes = sizes.at[source_of].add(-moved).at[receiver].add(moved)
    items = jnp.searchsorted(jnp.cumsum(sizes), jnp.arange(rows * top), side="right").astype(jnp.int32)
    listing = items.reshape(top, rows).T
    listing = listing[jax.random.permutation(jax.random.fold_in(own, 1), rows)]
    offset_by = jax.random.randint(jax.random.fold_in(own, 2), (rows, 1), 0, top)
    return jnp.take_along_axis(listing, (jnp.arange(top)[None, :] + offset_by) % top, axis=1)


def load_shares(number_of, total, most, skew, full):
    weights = [(1 << 20) // math.isqrt(grade ** skew) + 1 for grade in range(1, number_of + 1)]
    largest = most if full else min(most, max(-(-total // number_of), total * weights[0] // sum(weights)))
    least = 1 if total - largest >= number_of - 1 else 0
    holding, spare = [largest] + [least] * (number_of - 1), total - largest - least * (number_of - 1)
    while spare > 0:
        movable = [i for i in range(1, number_of) if holding[i] < largest] or [i for i in range(1, number_of) if holding[i] < most]
        whole, budget = sum([weights[i] for i in movable]), spare
        for i in movable:
            more = min(most - holding[i], max(1, budget * weights[i] // whole), spare)
            holding[i] = holding[i] + more
            spare = spare - more
    return np.array(holding)


def bell_draw(stream_key, shape, spread, bound, cuts=(), held_as=jnp.bfloat16):
    factor_of = block_scale(stream_key, shape, cuts, -0.22, 0.18) if cuts else 1.0
    result = jax.random.normal(stream_key, shape, jnp.float32) * spread * factor_of
    return jnp.minimum(jnp.maximum(result, -bound), bound).astype(held_as)


def setup_inputs(seed: int = 0) -> dict:
    arg_keys = jax.random.split(jax.random.key(seed), 8)
    hidden_states = bell_draw(arg_keys[0], (TOKENS, D), 1.0, 6.0, ((0, 128), (1, 8)))
    expert_ids_keys = jax.random.split(jax.random.fold_in(arg_keys[1], 1), TOKENS // TOK_G)
    expert_ids_turns = jax.random.permutation(jax.random.fold_in(arg_keys[1], 3), TOKENS // TOK_G)
    expert_ids = jax.vmap(lambda own, number: assign_block(jax.random.fold_in(arg_keys[1], 2), own, number, TOK_G, EXPERTS, TOP, CAP, 2))(expert_ids_keys, expert_ids_turns).reshape((TOKENS, TOP))
    gate_weights = jnp.clip(jnp.exp(math.log(0.3984375) - 2.5894505 * jax.random.uniform(arg_keys[2], (TOKENS, TOP), jnp.float32) ** block_scale(arg_keys[2], (TOKENS, TOP), ((0, 128),), -0.2, 0.2)), 0.029907227, 0.3984375).astype(jnp.bfloat16)
    completion_lengths = touch_ends(jax.random.randint(arg_keys[3], (COMPLETIONS,), SEQ // 8, SEQ + 1), jax.random.fold_in(arg_keys[3], 1), SEQ // 8, SEQ).astype(jnp.int32)
    output_grad = bell_draw(arg_keys[4], (TOKENS, D), 0.5, 3.0, ((0, 128), (1, 8)))
    gate_up_proj = bell_draw(arg_keys[5], (EXPERTS, 2, FF, D), D ** -0.5, 0.125, ((0, 32), (2, 8)))
    down_proj = bell_draw(arg_keys[6], (EXPERTS, FF, D), FF ** -0.5, 0.15625, ((0, 32), (1, 8)))
    return dict(hidden_states=hidden_states, expert_ids=expert_ids, gate_weights=gate_weights, completion_lengths=completion_lengths, output_grad=output_grad, gate_up_proj=gate_up_proj, down_proj=down_proj)


def silu_parts(pre_act):
    sigmoid_value = jax.nn.sigmoid(pre_act)
    return pre_act * sigmoid_value, sigmoid_value * (1.0 + pre_act * (1.0 - sigmoid_value))


def reference(hidden_states, expert_ids, gate_weights, completion_lengths, output_grad, gate_up_proj, down_proj):
    routes = TOKENS * TOP
    rows_max = N_EXPERT * CAP
    token_index = jnp.arange(TOKENS, dtype=jnp.int32)
    sample = token_index // SEQ
    keep_mask = ((token_index % SEQ) < completion_lengths[sample]).astype(jnp.float32)
    loss_scale = SEQ / completion_lengths.astype(jnp.float32)[sample]
    coefficient = gate_weights.astype(jnp.float32) * (keep_mask * loss_scale)[:, None]
    flat_ids = expert_ids.reshape(routes).astype(jnp.int32)
    route_token = jnp.arange(routes, dtype=jnp.int32) // TOP
    group_key = sample[route_token] * EXPERTS + flat_ids
    order = jnp.argsort(group_key, stable=True).astype(jnp.int32)
    sorted_key = group_key[order]
    counts = jnp.zeros((COMPLETIONS * EXPERTS,), jnp.int32).at[group_key].add(1)
    starts = jnp.cumsum(counts) - counts
    slot_place = jnp.arange(routes, dtype=jnp.int32) - starts[sorted_key]
    table = jnp.full((COMPLETIONS * EXPERTS, rows_max), routes, jnp.int32)
    table = table.at[sorted_key, slot_place].set(order)
    table = table.reshape(COMPLETIONS, EXPERTS, rows_max).transpose(1, 0, 2)
    padded_states = jnp.concatenate([hidden_states, jnp.zeros((1, D), jnp.bfloat16)], axis=0)
    padded_grad = jnp.concatenate([output_grad, jnp.zeros((1, D), jnp.bfloat16)], axis=0)
    padded_coef = jnp.concatenate([coefficient.reshape(routes), jnp.zeros((1,), jnp.float32)])

    def one_expert(operands):
        route_table, in_weight, out_weight = operands

        def one_group(route_list):
            valid = route_list < routes
            token_of = jnp.where(valid, route_list // TOP, TOKENS).astype(jnp.int32)
            inputs = padded_states[token_of]
            grad_rows = (padded_coef[route_list][:, None] * padded_grad[token_of].astype(jnp.float32)).astype(jnp.bfloat16)
            pre_gate = jnp.dot(inputs, in_weight[0].T, preferred_element_type=jnp.float32)
            pre_up = jnp.dot(inputs, in_weight[1].T, preferred_element_type=jnp.float32)
            activated, slope = silu_parts(pre_gate)
            hidden = (activated * pre_up).astype(jnp.bfloat16)
            hidden_grad = jnp.dot(grad_rows, out_weight.T, preferred_element_type=jnp.float32)
            gate_blocks = (hidden.astype(jnp.float32) * hidden_grad).reshape(rows_max, N_TENSOR, FFB).sum(axis=2).astype(jnp.bfloat16)
            gate_total = jnp.sum(lax.optimization_barrier(gate_blocks).astype(jnp.float32), axis=1).astype(jnp.bfloat16)
            act_gate = (hidden_grad * pre_up * slope).astype(jnp.bfloat16)
            act_up = (hidden_grad * activated).astype(jnp.bfloat16)
            row_blocks = jnp.einsum('msf,sfd->msd', act_gate.astype(jnp.float32).reshape(rows_max, N_TENSOR, FFB), in_weight[0].astype(jnp.float32).reshape(N_TENSOR, FFB, D), precision=lax.Precision.HIGHEST)
            row_blocks = row_blocks + jnp.einsum('msf,sfd->msd', act_up.astype(jnp.float32).reshape(rows_max, N_TENSOR, FFB), in_weight[1].astype(jnp.float32).reshape(N_TENSOR, FFB, D), precision=lax.Precision.HIGHEST)
            row_total = jnp.sum(lax.optimization_barrier(row_blocks.astype(jnp.bfloat16)).astype(jnp.float32), axis=1).astype(jnp.bfloat16)
            out_part = jnp.dot(hidden.T, grad_rows, preferred_element_type=jnp.float32)
            in_part = jnp.stack([jnp.dot(act_gate.T, inputs, preferred_element_type=jnp.float32), jnp.dot(act_up.T, inputs, preferred_element_type=jnp.float32)])
            return row_total, gate_total, in_part, out_part

        row_total, gate_total, in_part, out_part = lax.map(one_group, route_table)
        in_grad = jnp.sum(lax.optimization_barrier(in_part.astype(jnp.bfloat16)).astype(jnp.float32), axis=0).astype(jnp.bfloat16)
        out_grad = jnp.sum(lax.optimization_barrier(out_part.astype(jnp.bfloat16)).astype(jnp.float32), axis=0).astype(jnp.bfloat16)
        return row_total, gate_total, in_grad, out_grad

    rows_all, gates_all, gate_up_grad, down_grad = lax.map(one_expert, (table, gate_up_proj, down_proj))
    rows_all, gates_all = lax.optimization_barrier((rows_all, gates_all))
    flat_table = table.reshape(-1)
    token_of = jnp.where(flat_table < routes, flat_table // TOP, TOKENS).astype(jnp.int32)
    input_total = jnp.zeros((TOKENS + 1, D), jnp.float32).at[token_of].add(rows_all.reshape(-1, D).astype(jnp.float32))
    input_grad = input_total[:TOKENS].astype(jnp.bfloat16)
    gate_total = jnp.zeros((routes + 1,), jnp.float32).at[flat_table].add(gates_all.reshape(-1).astype(jnp.float32))
    gate_grad = gate_total[:routes].reshape(TOKENS, TOP) / gate_weights.astype(jnp.float32)
    return input_grad, gate_grad, gate_up_grad, down_grad
```

```python
import functools

import jax
import jax.numpy as jnp
from jax import lax
from jax.experimental import pallas as pl
from jax.experimental.pallas import tpu as pltpu
from jax.sharding import PartitionSpec as P

BF = jnp.bfloat16
F32 = jnp.float32
NY, NLO, NHI, NCORE = 4, 8, 4, 2
NZ = NLO * NHI
META = 128
NT_DIMS = (((1,), (1,)), ((), ()))
TN_DIMS = (((0,), (0,)), ((), ()))
PLANE = ("expert", "tensor")
VMEM = pl.BlockSpec(memory_space=pltpu.VMEM)
SMEM = pl.BlockSpec(memory_space=pltpu.SMEM)
LIMIT = 56 * 1024 * 1024


def place(y, z, core):
    return ((y * NLO + z % NLO) * NHI + z // NLO) * NCORE + core


def send(array, to):
    pairs = []
    for y in range(NY):
        for z in range(NZ):
            for core in range(NCORE):
                step = to(core)
                if step is None:
                    continue
                dy, dz, dcore = step
                there = place((y + dy) % NY, (z + dz) % NZ, (core + dcore) % NCORE)
                pairs.append((place(y, z, core), there))
    return lax.ppermute(array, PLANE, pairs)


def along_y(array, step):
    return send(array, lambda core: (step, 0, 0))


def along_z(array, step):
    return send(array, lambda core: (0, step, 0))


def to_other_core(array):
    return send(array, lambda core: (0, 0, 1))


def call(kernel, outs, *args, scalars=0, flops=0):
    moved = sum(a.size * a.dtype.itemsize for a in args)
    moved += sum(o.size * o.dtype.itemsize for o in outs)
    return pl.pallas_call(
        kernel,
        out_shape=outs,
        in_specs=[SMEM] * scalars + [VMEM] * (len(args) - scalars),
        out_specs=[VMEM] * len(outs),
        compiler_params=pltpu.CompilerParams(vmem_limit_bytes=LIMIT),
        cost_estimate=pl.CostEstimate(flops=flops, bytes_accessed=moved, transcendentals=0),
    )(*args)


def struct(shape, dtype=BF):
    return jax.ShapeDtypeStruct(shape, dtype)


def lanes(start, size):
    return pl.ds(pl.multiple_of(start, 128), size)


def gather_hi_kernel(where, own, before, after, across, out):
    hi = where[2]
    width = own.shape[1] // 2
    for block, step in ((own, 0), (before, NHI - 1), (after, 1), (across, 2)):
        at = ((hi + step) % NHI) * width
        out[:, lanes(at, width)] = block[:, :width]
        out[:, lanes(NHI * width + at, width)] = block[:, width:]


def gather_core_kernel(where, own, other, ids, weights, rows, grads):
    core = where[3]
    half = own.shape[1] // 2
    width = half // NHI
    for block, side in ((own, core), (other, 1 - core)):
        for hi in range(NHI):
            at = (hi * NCORE + side) * width
            rows[:, lanes(at, width)] = block[:, hi * width : (hi + 1) * width]
            grads[:, lanes(at, width)] = block[:, half + hi * width : half + (hi + 1) * width]
    top = ids.shape[1]
    lane = lax.broadcasted_iota(jnp.int32, (top, META), 1)
    row = lax.broadcasted_iota(jnp.int32, (top, META), 0)
    spread_ids = (lane == row).astype(F32).astype(BF)
    spread_weights = (lane == row + top).astype(F32).astype(BF)
    meta = jnp.dot(ids[...].astype(F32).astype(BF), spread_ids, preferred_element_type=F32)
    meta += jnp.dot(weights[...], spread_weights, preferred_element_type=F32)
    rows[:, 2 * half :] = meta.astype(BF)


def group_rows(core, received, fourth, own):
    blocks = [r[...] for r in received]
    last = jnp.where(core == 0, fourth[...].astype(F32), own[...].astype(F32)).astype(BF)
    return jnp.concatenate(blocks + [last], axis=0)


def select_rows_kernel(where, scale, first, second, third, fourth, own, *outs):
    sends, (placing, coefs, metas) = outs[:NY], outs[NY:]
    y, lo, core, length = where[0], where[1], where[3], where[4]
    tokens = own.shape[0]
    features = own.shape[1] - META
    total = placing.shape[1]
    slots = total // (NY * 2 * 4)
    blocks = group_rows(core, (first, second, third), fourth, own)
    meta = blocks[:, features:].astype(F32)
    metas[...] = meta
    slot = lax.broadcasted_iota(jnp.int32, (tokens, total), 1)
    expert = ((((y + slot // (8 * slots)) % NY) * NLO + lo) * 2 + (slot // (4 * slots)) % 2).astype(F32)
    rank_of = (slot % slots).astype(F32)
    group_of = (slot // slots) % 4
    token = lax.broadcasted_iota(jnp.int32, (tokens, total), 0)
    lower = (
        lax.broadcasted_iota(jnp.int32, (tokens, tokens), 0)
        >= lax.broadcasted_iota(jnp.int32, (tokens, tokens), 1)
    ).astype(F32).astype(BF)
    parts, weighted = [], []
    for group in range(4):
        named = meta[group * tokens : (group + 1) * tokens]
        hit = jnp.zeros((tokens, total), F32)
        weight = jnp.zeros((tokens, total), F32)
        for k in range(8):
            same = named[:, k : k + 1] == expert
            hit += same.astype(F32)
            weight += jnp.where(same, named[:, 8 + k : 9 + k], 0.0)
        hit = jnp.where(group_of == group, hit, 0.0)
        rank = jnp.dot(lower, hit.astype(BF), preferred_element_type=F32)
        placed = jnp.where(rank == rank_of + 1.0, hit, 0.0)
        step = group + 1
        offset = jnp.where(core == 0, -step, step if group < 3 else 0)
        position = (y * NLO + (lo + offset + NLO) % NLO) * tokens + token
        parts.append(placed)
        weighted.append(jnp.where(position < length, placed * weight, 0.0))
    place_matrix = jnp.concatenate(parts, axis=0).astype(BF)
    weight_matrix = jnp.concatenate(weighted, axis=0).astype(BF)
    placing[...] = place_matrix
    ones = jnp.ones((4 * tokens, META), BF)
    coefs[...] = lax.dot_general(weight_matrix, ones, TN_DIMS, preferred_element_type=F32) * scale[0]
    chosen = lax.dot_general(
        place_matrix, blocks[:, :features], TN_DIMS, preferred_element_type=F32
    ).astype(BF)
    share = total // NY
    for step in range(NY):
        sends[step][...] = chosen[step * share : (step + 1) * share]


def select_grads_kernel(where, placing, coefs, first, second, third, fourth, own, *sends):
    blocks = group_rows(where[3], (first, second, third), fourth, own)
    chosen = lax.dot_general(placing[...], blocks, TN_DIMS, preferred_element_type=F32)
    chosen = (chosen * coefs[:, :1]).astype(BF)
    share = placing.shape[1] // NY
    for step in range(NY):
        sends[step][...] = chosen[step * share : (step + 1) * share]


def of_expert(array, expert, share):
    half = share // 2
    return jnp.concatenate(
        [
            array[step * share + expert * half : step * share + (expert + 1) * half]
            for step in range(NY)
        ],
        axis=0,
    )


def expert_kernel(rows, grads, gate_up, down, gate_up_other, down_other, *outs):
    returns, (acts, acts_other) = outs[:NY], outs[NY:]
    share = rows.shape[0] // NY
    half = share // 2
    features = rows.shape[1]
    lane = lax.broadcasted_iota(jnp.int32, (half, META), 1)
    for expert in range(2):
        inputs = of_expert(rows, expert, share)
        cotangents = of_expert(grads, expert, share)
        back = jnp.zeros((NY * half, features), F32)
        gate = jnp.zeros((NY * half, 1), F32)
        for w_in, w_out, acts_here in ((gate_up, down, acts), (gate_up_other, down_other, acts_other)):
            w_gate, w_up = w_in[expert, 0], w_in[expert, 1]
            pre_gate = lax.dot_general(inputs, w_gate, NT_DIMS, preferred_element_type=F32)
            pre_up = lax.dot_general(inputs, w_up, NT_DIMS, preferred_element_type=F32)
            hidden_grad = lax.dot_general(cotangents, w_out[expert], NT_DIMS, preferred_element_type=F32)
            sigmoid = jax.nn.sigmoid(pre_gate)
            active = pre_gate * sigmoid
            slope = sigmoid * (1.0 + pre_gate * (1.0 - sigmoid))
            hidden = (active * pre_up).astype(BF)
            gate += jnp.sum(hidden.astype(F32) * hidden_grad, axis=1, keepdims=True)
            act_gate = (hidden_grad * pre_up * slope).astype(BF)
            act_up = (hidden_grad * active).astype(BF)
            acts_here[expert, 0] = act_gate
            acts_here[expert, 1] = act_up
            acts_here[expert, 2] = hidden
            back += jnp.dot(act_gate, w_gate, preferred_element_type=F32)
            back += jnp.dot(act_up, w_up, preferred_element_type=F32)
        back = back.astype(BF)
        for step in range(NY):
            here = slice(expert * half, (expert + 1) * half)
            there = slice(step * half, (step + 1) * half)
            returns[step][here, :features] = back[there]
            returns[step][here, features:] = jnp.where(lane == step * 2 + expert, gate[there], 0.0).astype(BF)


def weight_grad_kernel(rows, rows_other, grads, grads_other, acts, acts_other, out):
    share = rows.shape[0] // NY
    units = acts.shape[3]
    for expert in range(2):
        inputs = jnp.concatenate(
            [of_expert(rows, expert, share), of_expert(rows_other, expert, share)], axis=0
        )
        cotangents = jnp.concatenate(
            [of_expert(grads, expert, share), of_expert(grads_other, expert, share)], axis=0
        )
        for which, right, at in (
            (0, inputs, expert * 2 * units),
            (1, inputs, (expert * 2 + 1) * units),
            (2, cotangents, (4 + expert) * units),
        ):
            left = jnp.concatenate([acts[expert, which], acts_other[expert, which]], axis=0)
            out[at : at + units] = lax.dot_general(
                left, right, TN_DIMS, preferred_element_type=F32
            ).astype(BF)


def combine_kernel(where, placing, metas, first, second, third, fourth, *outs):
    y, lo = where[0], where[1]
    features = first.shape[1] - META
    width = features // (NHI * NCORE)
    back = jnp.concatenate([first[...], second[...], third[...], fourth[...]], axis=0)
    summed = jnp.dot(placing[...], back, preferred_element_type=F32)
    meta = metas[...]
    lane = lax.broadcasted_iota(jnp.int32, meta.shape, 1)
    gate = jnp.zeros(meta.shape, F32)
    for step in range(NY):
        for j in range(2):
            expert = (((y + step) % NY) * NLO + lo) * 2 + j
            at = features + step * 2 + j
            same = jnp.logical_and(meta == expert.astype(F32), lane < 8)
            gate += jnp.where(same, summed[:, at : at + 1], 0.0)
    gate = gate.astype(BF)
    tokens = outs[0].shape[0]
    for group in range(4):
        here = slice(group * tokens, (group + 1) * tokens)
        for core in range(NCORE):
            for hi in range(NHI):
                there = (hi * NCORE + core) * width
                at = (core * NHI + hi) * width
                outs[group][:, at : at + width] = summed[here, there : there + width].astype(BF)
        outs[group][:, features:] = gate[here]


def split_core_kernel(where, arrived, own, keep, give):
    core = where[3]
    half = (arrived.shape[1] - META) // 2
    mine = jnp.where(core == 1, 1.0, 0.0)
    for out, side in ((keep, core), (give, 1 - core)):
        at = lanes(side * half, half)
        out[:, :half] = (arrived[:, at].astype(F32) + mine * own[:, at].astype(F32)).astype(BF)
        out[:, half:] = (arrived[:, 2 * half :].astype(F32) + mine * own[:, 2 * half :].astype(F32)).astype(BF)


def split_hi_kernel(where, kept, arrived, *outs):
    hi = where[2]
    half = kept.shape[1] - META
    width = half // NHI
    gate = (kept[:, half:].astype(F32) + arrived[:, half:].astype(F32)).astype(BF)
    for step in range(NHI):
        at = lanes(((hi + step) % NHI) * width, width)
        outs[step][:, :width] = (kept[:, at].astype(F32) + arrived[:, at].astype(F32)).astype(BF)
        outs[step][:, width:] = gate


def finish_kernel(where, weights, own, before, after, across, input_grad, gate_grad):
    column = where[2] * NCORE + where[3]
    width = own.shape[1] - META
    total = own[...].astype(F32) + before[...].astype(F32)
    total += after[...].astype(F32) + across[...].astype(F32)
    input_grad[...] = total[:, :width].astype(BF)
    gate = total[:, width:]
    lane = lax.broadcasted_iota(jnp.int32, gate.shape, 1)
    route = lax.broadcasted_iota(jnp.int32, weights.shape, 1)
    top = jnp.sum(jnp.where(lane == column, gate, 0.0), axis=1, keepdims=True)
    under = jnp.sum(jnp.where(route == column, weights[...].astype(F32), 0.0), axis=1, keepdims=True)
    gate_grad[...] = top / under


def local(
    hidden_states,
    expert_ids,
    gate_weights,
    completion_lengths,
    output_grad,
    gate_up_proj,
    down_proj,
):
    tokens, width = hidden_states.shape
    features = width * NHI * NCORE
    units = gate_up_proj.shape[2]
    slots = tokens * expert_ids.shape[1] // (NY * NLO * 2)
    total = NY * 2 * 4 * slots
    share = total // NY
    expert_at, tensor_at = lax.axis_index("expert"), lax.axis_index("tensor")
    length = completion_lengths[0]
    where = jnp.stack(
        [expert_at // NLO, expert_at % NLO, tensor_at // NCORE, tensor_at % NCORE, length]
    ).astype(jnp.int32)
    scale = ((tokens * NY * NLO) / completion_lengths.astype(F32)).astype(F32)

    own = jnp.concatenate([hidden_states, output_grad], axis=1)
    before, after, across = along_z(own, NLO), along_z(own, -NLO), along_z(own, 2 * NLO)
    gate_up_other, down_other = to_other_core(gate_up_proj), to_other_core(down_proj)
    (half,) = call(
        gather_hi_kernel,
        [struct((tokens, 2 * NHI * width))],
        where, own, before, after, across, scalars=1,
    )
    rows, grads = call(
        gather_core_kernel,
        [struct((tokens, features + META)), struct((tokens, features))],
        where, half, to_other_core(half), expert_ids, gate_weights, scalars=1,
    )

    def onward(block):
        got, passed = [], block
        for _ in range(3):
            passed = send(passed, lambda core: (0, 1 if core == 0 else -1, 0))
            got.append(passed)
        got.append(send(passed, lambda core: (0, 1, 0) if core == 0 else None))
        return got

    row_blocks, grad_blocks = onward(rows), onward(grads)
    *row_sends, placing, coefs, metas = call(
        select_rows_kernel,
        [struct((share, features))] * NY
        + [struct((4 * tokens, total)), struct((total, META), F32), struct((4 * tokens, META), F32)],
        where, scale, *row_blocks, rows, scalars=2, flops=2 * 4 * tokens * total * features,
    )
    grad_sends = call(
        select_grads_kernel,
        [struct((share, features))] * NY,
        where, placing, coefs, *grad_blocks, grads, scalars=1, flops=2 * 4 * tokens * total * features,
    )

    def over_y(blocks, sign):
        return [blocks[0]] + [along_y(blocks[step], sign * step) for step in range(1, NY)]

    expert_rows = jnp.concatenate(over_y(row_sends, 1), axis=0)
    expert_grads = jnp.concatenate(over_y(grad_sends, 1), axis=0)
    rows_other, grads_other = to_other_core(expert_rows), to_other_core(expert_grads)
    acts_shape = struct((2, 3, total // 2, units))
    *returns, acts, acts_theirs = call(
        expert_kernel,
        [struct((share, features + META))] * NY + [acts_shape, acts_shape],
        expert_rows, expert_grads, gate_up_proj, down_proj, gate_up_other, down_other,
        flops=2 * total * 2 * units * features * 5,
    )
    acts_other = to_other_core(acts_theirs)
    returned = over_y(returns, -1)
    (weight_parts,) = call(
        weight_grad_kernel,
        [struct((6 * units, features))],
        expert_rows, rows_other, expert_grads, grads_other, acts, acts_other,
        flops=2 * 2 * total * units * features * 3,
    )
    weight_grads = lax.psum_scatter(weight_parts, "dp", scatter_dimension=1, tiled=True)

    sums = call(
        combine_kernel,
        [struct((tokens, features + META))] * 4,
        where, placing, metas, *returned, scalars=1, flops=2 * 4 * tokens * total * features,
    )
    passed = send(sums[3], lambda core: (0, -1, 0) if core == 0 else None)
    for group in (2, 1, 0):
        passed = (passed.astype(F32) + sums[group].astype(F32)).astype(BF)
        passed = send(passed, lambda core: (0, -1 if core == 0 else 1, 0))
    half_shape = struct((tokens, features // 2 + META))
    keep, give = call(split_core_kernel, [half_shape, half_shape], where, passed, sums[3], scalars=1)
    pieces = call(
        split_hi_kernel,
        [struct((tokens, width + META))] * NHI,
        where, keep, to_other_core(give), scalars=1,
    )
    input_grad, gate_grad = call(
        finish_kernel,
        [struct((tokens, width)), struct((tokens, 1), F32)],
        where,
        gate_weights,
        pieces[0],
        along_z(pieces[1], NLO),
        along_z(pieces[3], -NLO),
        along_z(pieces[2], 2 * NLO),
        scalars=1,
    )
    part = weight_grads.shape[1]
    gate_up_grad = weight_grads[: 4 * units].reshape(2, 2, units, part)
    down_grad = weight_grads[4 * units :].reshape(2, units, part)
    return (input_grad, gate_grad, gate_up_grad, down_grad)


def solution(mesh):
    placed = (
        P(("dp", "expert"), "tensor"),
        P(("dp", "expert"), None),
        P(("dp", "expert"), None),
        P("dp"),
        P(("dp", "expert"), "tensor"),
        P("expert", None, "tensor", None),
        P("expert", "tensor", None),
    )
    return jax.shard_map(
        local,
        mesh=mesh,
        in_specs=placed,
        out_specs=(
            P(("dp", "expert"), "tensor"),
            P(("dp", "expert"), "tensor"),
            P("expert", None, "tensor", "dp"),
            P("expert", "tensor", "dp"),
        ),
        check_vma=False,
    )
```

```python
import functools

import jax
import jax.numpy as jnp
from jax import lax
from jax.experimental import pallas as pl
from jax.experimental.pallas import tpu as pltpu
from jax.sharding import PartitionSpec as P

BF = jnp.bfloat16
F32 = jnp.float32
NY, NLO, NHI, NCORE = 4, 8, 4, 2
NZ = NLO * NHI
META = 128
NT_DIMS = (((1,), (1,)), ((), ()))
TN_DIMS = (((0,), (0,)), ((), ()))
PLANE = ("expert", "tensor")
VMEM = pl.BlockSpec(memory_space=pltpu.VMEM)
SMEM = pl.BlockSpec(memory_space=pltpu.SMEM)
LIMIT = 56 * 1024 * 1024


def place(y, z, core):
    return ((y * NLO + z % NLO) * NHI + z // NLO) * NCORE + core


def send(array, to):
    pairs = []
    for y in range(NY):
        for z in range(NZ):
            for core in range(NCORE):
                step = to(core)
                if step is None:
                    continue
                dy, dz, dcore = step
                there = place((y + dy) % NY, (z + dz) % NZ, (core + dcore) % NCORE)
                pairs.append((place(y, z, core), there))
    return lax.ppermute(array, PLANE, pairs)


def swap_y(array):
    groups = [[y * NLO + lo for y in range(NY)] for lo in range(NLO)]
    return lax.all_to_all(
        array, "expert", split_axis=0, concat_axis=0, tiled=True, axis_index_groups=groups
    )


def swap_hi(array):
    groups = [[hi * NCORE + core for hi in range(NHI)] for core in range(NCORE)]
    return lax.all_to_all(
        array, "tensor", split_axis=0, concat_axis=0, tiled=True, axis_index_groups=groups
    )


def to_other_core(array):
    return send(array, lambda core: (0, 0, 1))


def call(kernel, outs, *args, scalars=0, flops=0):
    moved = sum(a.size * a.dtype.itemsize for a in args)
    moved += sum(o.size * o.dtype.itemsize for o in outs)
    return pl.pallas_call(
        kernel,
        out_shape=outs,
        in_specs=[SMEM] * scalars + [VMEM] * (len(args) - scalars),
        out_specs=[VMEM] * len(outs),
        compiler_params=pltpu.CompilerParams(vmem_limit_bytes=LIMIT),
        cost_estimate=pl.CostEstimate(flops=flops, bytes_accessed=moved, transcendentals=0),
    )(*args)


def struct(shape, dtype=BF):
    return jax.ShapeDtypeStruct(shape, dtype)


def eye(size):
    row = lax.broadcasted_iota(jnp.int32, (size, size), 0)
    column = lax.broadcasted_iota(jnp.int32, (size, size), 1)
    return (row == column).astype(F32).astype(BF)


def group_blocks(core, received, fourth, own):
    last = jnp.where(core == 0, fourth[...].astype(F32), own[...].astype(F32)).astype(BF)
    return [r[...] for r in received] + [last]


def select_kernel(where, scale, *refs):
    row_refs, grad_refs, (sends, placing, metas) = refs[:5], refs[5:10], refs[10:]
    y, lo, core, length = where[0], where[1], where[3], where[4]
    parts = NHI * NCORE
    tokens = grad_refs[0].shape[0] // parts
    width = grad_refs[0].shape[1]
    total = placing.shape[0]
    share = total // NY
    slots = share // 8
    rows = group_blocks(core, row_refs[:3], row_refs[3], row_refs[4])
    grads = group_blocks(core, grad_refs[:3], grad_refs[3], grad_refs[4])
    slot = lax.broadcasted_iota(jnp.int32, (tokens, total), 1)
    expert = (((slot // share) * NLO + lo) * 2 + (slot // (4 * slots)) % 2).astype(F32)
    rank_of = (slot % slots).astype(F32)
    group_of = (slot // slots) % 4
    token = lax.broadcasted_iota(jnp.int32, (tokens, total), 0)
    lower = (
        lax.broadcasted_iota(jnp.int32, (tokens, tokens), 0)
        >= lax.broadcasted_iota(jnp.int32, (tokens, tokens), 1)
    ).astype(F32).astype(BF)
    placed_parts, weighted = [], []
    for group in range(4):
        packed = rows[group][parts * tokens :, :tokens]
        named = lax.dot_general(eye(tokens), packed, NT_DIMS, preferred_element_type=F32)
        metas[group * tokens : (group + 1) * tokens] = named
        hit = jnp.zeros((tokens, total), F32)
        weight = jnp.zeros((tokens, total), F32)
        for k in range(8):
            same = named[:, k : k + 1] == expert
            hit += same.astype(F32)
            weight += jnp.where(same, named[:, 8 + k : 9 + k], 0.0)
        hit = jnp.where(group_of == group, hit, 0.0)
        rank = jnp.dot(lower, hit.astype(BF), preferred_element_type=F32)
        placed = jnp.where(rank == rank_of + 1.0, hit, 0.0)
        step = group + 1
        offset = jnp.where(core == 0, -step, step if group < 3 else 0)
        position = (y * NLO + (lo + offset + NLO) % NLO) * tokens + token
        placed_parts.append(placed)
        weighted.append(jnp.where(position < length, placed * weight, 0.0))
    matrix = jnp.concatenate(placed_parts, axis=0).T.astype(BF)
    weight_matrix = jnp.concatenate(weighted, axis=0).astype(BF)
    placing[...] = matrix
    ones = jnp.ones((4 * tokens, width), BF)
    coefs = lax.dot_general(weight_matrix, ones, TN_DIMS, preferred_element_type=F32) * scale[0]
    for blocks, start in ((rows, 0), (grads, parts * width)):
        for part in range(parts):
            here = jnp.concatenate([b[part * tokens : (part + 1) * tokens] for b in blocks], axis=0)
            chosen = jnp.dot(matrix, here, preferred_element_type=F32)
            if start:
                chosen = chosen * coefs
            chosen = chosen.astype(BF)
            at = start + part * width
            for step in range(NY):
                sends[step, :, at : at + width] = chosen[step * share : (step + 1) * share]


def of_expert(routes, expert, start, size):
    half = routes.shape[1] // 2
    here = slice(expert * half, (expert + 1) * half)
    return jnp.concatenate([routes[step, here, start : start + size] for step in range(NY)], axis=0)


def expert_kernel(where, routes, gate_up, down, gate_up_other, down_other, returns, acts, acts_other):
    half = routes.shape[1] // 2
    features = routes.shape[2] // 2
    y = where[0]
    units = down.shape[1]
    lane = lax.broadcasted_iota(jnp.int32, (half, META), 1)
    for expert in range(2):
        inputs = of_expert(routes, expert, 0, features).T
        cotangents = of_expert(routes, expert, features, features).T
        back = jnp.zeros((NY * half, features), F32)
        gate = jnp.zeros((1, NY * half), F32)
        for w_in, w_out, acts_here in ((gate_up, down, acts), (gate_up_other, down_other, acts_other)):
            w_gate, w_up = w_in[expert, 0], w_in[expert, 1]
            pre_gate = jnp.dot(w_gate, inputs, preferred_element_type=F32)
            pre_up = jnp.dot(w_up, inputs, preferred_element_type=F32)
            hidden_grad = jnp.dot(w_out[expert], cotangents, preferred_element_type=F32)
            sigmoid = jax.nn.sigmoid(pre_gate)
            active = pre_gate * sigmoid
            slope = sigmoid * (1.0 + pre_gate * (1.0 - sigmoid))
            hidden = (active * pre_up).astype(BF)
            gate += jnp.sum(hidden.astype(F32) * hidden_grad, axis=0, keepdims=True)
            act_gate = (hidden_grad * pre_up * slope).astype(BF)
            act_up = (hidden_grad * active).astype(BF)
            acts_here[expert, 0] = act_gate
            acts_here[expert, 1] = act_up
            acts_here[expert, 2] = hidden
            back += lax.dot_general(act_gate, w_gate, TN_DIMS, preferred_element_type=F32)
            back += lax.dot_general(act_up, w_up, TN_DIMS, preferred_element_type=F32)
        back = back.astype(BF)
        gate_rows = jnp.broadcast_to(gate, (META, NY * half)).astype(BF)
        gate_columns = lax.dot_general(eye(NY * half), gate_rows, NT_DIMS, preferred_element_type=F32)
        for step in range(NY):
            here = slice(expert * half, (expert + 1) * half)
            there = slice(step * half, (step + 1) * half)
            returns[step, here, :features] = back[there]
            returns[step, here, features:] = jnp.where(
                lane == y * 2 + expert, gate_columns[there], 0.0
            ).astype(BF)


def weight_grad_kernel(routes, routes_other, acts, acts_other, out):
    units = acts.shape[2]
    features = routes.shape[2] // 2

    def both(expert, start):
        pieces = [of_expert(r, expert, start, features) for r in (routes, routes_other)]
        return jnp.concatenate(pieces, axis=0)

    for expert in range(2):
        inputs = both(expert, 0)
        cotangents = both(expert, features)
        for which, right, at in (
            (0, inputs, expert * 2 * units),
            (1, inputs, (expert * 2 + 1) * units),
            (2, cotangents, (4 + expert) * units),
        ):
            left = jnp.concatenate([acts[expert, which], acts_other[expert, which]], axis=1)
            out[at : at + units] = jnp.dot(left, right, preferred_element_type=F32).astype(BF)


def combine_kernel(where, placing, metas, returned, *outs):
    lo, core = where[1], where[3]
    features = returned.shape[2] - META
    back = jnp.concatenate([returned[step] for step in range(NY)], axis=0)
    summed = lax.dot_general(placing[...], back, TN_DIMS, preferred_element_type=F32)
    named = metas[:, :8]
    gate = jnp.zeros(named.shape, F32)
    for step in range(NY):
        for j in range(2):
            expert = (step * NLO + lo) * 2 + j
            at = features + step * 2 + j
            gate += jnp.where(named == expert.astype(F32), summed[:, at : at + 1], 0.0)
    tokens = outs[0].shape[0]
    for out, up, other in zip(outs, (3, 2, 1, 0), (2, 1, 0, 3), strict=True):
        a, b = (slice(g * tokens, (g + 1) * tokens) for g in (up, other))
        out[:, :features] = jnp.where(core == 0, summed[a, :features], summed[b, :features]).astype(BF)
        out[:, features:] = jnp.zeros((tokens, META), BF)
        out[:, features : features + 8] = jnp.where(core == 0, gate[a], gate[b]).astype(BF)


def split_core_kernel(where, arrived, below, kept, keep, give):
    tokens, features = arrived.shape[0], arrived.shape[1] - META
    width = features // (NHI * NCORE)
    first = where[3] == 0
    last = jnp.where(first, below[...].astype(F32), kept[...].astype(F32))
    total = arrived[...].astype(F32) + last
    gate = lax.dot_general(total[:, features:].astype(BF), eye(tokens), TN_DIMS, preferred_element_type=F32)
    for hi in range(NHI):
        blocks = []
        for part in (hi * NCORE, hi * NCORE + 1):
            row = jnp.broadcast_to(gate[part : part + 1], (16, tokens))
            blocks.append((total[:, part * width : (part + 1) * width], row))
        (zero, zero_gate), (one, one_gate) = blocks
        for out, swap in ((keep, first), (give, jnp.logical_not(first))):
            out[hi, :tokens] = jnp.where(swap, zero, one).astype(BF)
            out[hi, tokens:] = jnp.zeros((16, width), BF)
            out[hi, tokens:, :tokens] = jnp.where(swap, zero_gate, one_gate).astype(BF)


def finish_kernel(where, weights, pieces, input_grad, gate_grad):
    column = where[2] * NCORE + where[3]
    tokens = input_grad.shape[0]
    total = pieces[0].astype(F32)
    for hi in range(1, NHI):
        total += pieces[hi].astype(F32)
    input_grad[...] = total[:tokens].astype(BF)
    route = lax.broadcasted_iota(jnp.int32, weights.shape, 0)
    under = jnp.sum(jnp.where(route == column, weights[...].astype(F32), 0.0), axis=0, keepdims=True)
    gate_grad[...] = total[tokens : tokens + 1, :tokens] / under


def local(
    hidden_states,
    expert_ids,
    gate_weights,
    completion_lengths,
    output_grad,
    gate_up_proj,
    down_proj,
):
    tokens, width = hidden_states.shape
    parts = NHI * NCORE
    features = width * parts
    units = gate_up_proj.shape[2]
    slots = tokens * expert_ids.shape[1] // (NY * NLO * 2)
    total = NY * 2 * 4 * slots
    share = total // NY
    expert_at, tensor_at = lax.axis_index("expert"), lax.axis_index("tensor")
    where = jnp.stack(
        [
            expert_at // NLO,
            expert_at % NLO,
            tensor_at // NCORE,
            tensor_at % NCORE,
            completion_lengths[0],
        ]
    ).astype(jnp.int32)
    scale = ((tokens * NY * NLO) / completion_lengths.astype(F32)).astype(F32)
    weights_across = gate_weights.T
    meta = jnp.concatenate([expert_ids.T.astype(F32).astype(BF), weights_across], axis=0)
    meta = jnp.pad(meta, ((0, 0), (0, width - tokens)))

    gathered = lax.all_gather(
        jnp.concatenate([hidden_states, output_grad], axis=1), "tensor", axis=0, tiled=True
    )
    gate_up_other, down_other = to_other_core(gate_up_proj), to_other_core(down_proj)
    rows = jnp.concatenate([gathered[:, :width], meta], axis=0)
    grads = gathered[:, width:]

    def onward(block):
        return send(block, lambda core: (0, 1 if core == 0 else -1, 0))

    def onward_last(block):
        return send(block, lambda core: (0, 1, 0) if core == 0 else None)

    row_blocks, grad_blocks = [rows], [grads]
    for _ in range(3):
        row_blocks.append(onward(row_blocks[-1]))
        grad_blocks.append(onward(grad_blocks[-1]))
    row_blocks = row_blocks[1:] + [onward_last(row_blocks[-1])]
    grad_blocks = grad_blocks[1:] + [onward_last(grad_blocks[-1])]
    sends, placing, metas = call(
        select_kernel,
        [
            struct((NY, share, 2 * features)),
            struct((total, 4 * tokens)),
            struct((4 * tokens, 16), F32),
        ],
        where, scale, *row_blocks, rows, *grad_blocks, grads,
        scalars=2, flops=4 * 4 * tokens * total * features,
    )
    routes = swap_y(sends)
    routes_other = to_other_core(routes)
    acts_shape = struct((2, 3, units, total // 2))
    returns, acts, acts_theirs = call(
        expert_kernel,
        [struct((NY, share, features + META)), acts_shape, acts_shape],
        where, routes, gate_up_proj, down_proj, gate_up_other, down_other,
        scalars=1, flops=2 * total * 2 * units * features * 5,
    )
    acts_other = to_other_core(acts_theirs)
    returned = swap_y(returns)
    (weight_parts,) = call(
        weight_grad_kernel,
        [struct((6 * units, features))],
        routes, routes_other, acts, acts_other,
        flops=2 * 2 * total * units * features * 3,
    )
    weight_grads = lax.psum_scatter(weight_parts, "dp", scatter_dimension=1, tiled=True)

    far, next_far, near, last = call(
        combine_kernel,
        [struct((tokens, features + META))] * 4,
        where, placing, metas, returned, scalars=1, flops=2 * 4 * tokens * total * features,
    )

    def two_back(block):
        return send(block, lambda core: (0, -2 if core == 0 else 2, 0))

    def add(one, other):
        return (one.astype(F32) + other.astype(F32)).astype(BF)

    near = add(near, two_back(far))
    last = add(last, two_back(next_far))
    arrived = send(near, lambda core: (0, -2 if core == 0 else 1, 0))
    below = send(last, lambda core: (0, -1, 0) if core == 0 else None)
    keep, give = call(
        split_core_kernel,
        [struct((NHI, tokens + 16, width))] * 2,
        where, arrived, below, last, scalars=1,
    )
    pieces = swap_hi(add(keep, to_other_core(give)))
    input_grad, gate_grad = call(
        finish_kernel,
        [struct((tokens, width)), struct((1, tokens), F32)],
        where, weights_across, pieces, scalars=1,
    )
    part = weight_grads.shape[1]
    gate_up_grad = weight_grads[: 4 * units].reshape(2, 2, units, part)
    down_grad = weight_grads[4 * units :].reshape(2, units, part)
    return (input_grad, gate_grad.reshape(tokens, 1), gate_up_grad, down_grad)


def solution(mesh):
    placed = (
        P(("dp", "expert"), "tensor"),
        P(("dp", "expert"), None),
        P(("dp", "expert"), None),
        P("dp"),
        P(("dp", "expert"), "tensor"),
        P("expert", None, "tensor", None),
        P("expert", "tensor", None),
    )
    return jax.shard_map(
        local,
        mesh=mesh,
        in_specs=placed,
        out_specs=(
            P(("dp", "expert"), "tensor"),
            P(("dp", "expert"), "tensor"),
            P("expert", None, "tensor", "dp"),
            P("expert", "tensor", "dp"),
        ),
        check_vma=False,
    )
```

```python
import functools

import jax
import jax.numpy as jnp
from jax import lax
from jax.experimental import pallas as pl
from jax.experimental.pallas import tpu as pltpu
from jax.sharding import PartitionSpec as P

BF = jnp.bfloat16
F32 = jnp.float32
NY, NLO, NHI, NCORE = 4, 8, 4, 2
NZ = NLO * NHI
META = 128
NT_DIMS = (((1,), (1,)), ((), ()))
TN_DIMS = (((0,), (0,)), ((), ()))
PLANE = ("expert", "tensor")
VMEM = pl.BlockSpec(memory_space=pltpu.VMEM)
SMEM = pl.BlockSpec(memory_space=pltpu.SMEM)
LIMIT = 56 * 1024 * 1024


def place(y, z, core):
    return ((y * NLO + z % NLO) * NHI + z // NLO) * NCORE + core


def send(array, to):
    pairs = []
    for y in range(NY):
        for z in range(NZ):
            for core in range(NCORE):
                step = to(core)
                if step is None:
                    continue
                dy, dz, dcore = step
                there = place((y + dy) % NY, (z + dz) % NZ, (core + dcore) % NCORE)
                pairs.append((place(y, z, core), there))
    return lax.ppermute(array, PLANE, pairs)


def swap_y(array):
    groups = [[y * NLO + lo for y in range(NY)] for lo in range(NLO)]
    return lax.all_to_all(
        array, "expert", split_axis=0, concat_axis=0, tiled=True, axis_index_groups=groups
    )


def swap_hi(array):
    groups = [[hi * NCORE + core for hi in range(NHI)] for core in range(NCORE)]
    return lax.all_to_all(
        array, "tensor", split_axis=0, concat_axis=0, tiled=True, axis_index_groups=groups
    )


def to_other_core(array):
    return send(array, lambda core: (0, 0, 1))


def call(kernel, outs, *args, scalars=0, flops=0):
    moved = sum(a.size * a.dtype.itemsize for a in args)
    moved += sum(o.size * o.dtype.itemsize for o in outs)
    ins = [SMEM if i < scalars else VMEM for i in range(len(args))]
    return pl.pallas_call(
        kernel,
        out_shape=outs,
        in_specs=ins,
        out_specs=[VMEM] * len(outs),
        compiler_params=pltpu.CompilerParams(vmem_limit_bytes=LIMIT),
        cost_estimate=pl.CostEstimate(flops=flops, bytes_accessed=moved, transcendentals=0),
    )(*args)


def struct(shape, dtype=BF):
    return jax.ShapeDtypeStruct(shape, dtype)


def eye(size):
    row = lax.broadcasted_iota(jnp.int32, (size, size), 0)
    column = lax.broadcasted_iota(jnp.int32, (size, size), 1)
    return (row == column).astype(F32).astype(BF)


def group_blocks(core, received, fourth, own):
    last = jnp.where(core == 0, fourth[...].astype(F32), own[...].astype(F32)).astype(BF)
    return [r[...] for r in received] + [last]


def select_kernel(where, scale, *refs):
    row_refs, grad_refs, (sends, placing, metas) = refs[:5], refs[5:10], refs[10:]
    y, lo, core, length = where[0], where[1], where[3], where[4]
    parts = NHI * NCORE
    tokens = grad_refs[0].shape[0] // parts
    width = grad_refs[0].shape[1]
    total = placing.shape[0]
    share = total // NY
    slots = share // 8
    rows = group_blocks(core, row_refs[:3], row_refs[3], row_refs[4])
    grads = group_blocks(core, grad_refs[:3], grad_refs[3], grad_refs[4])
    slot = lax.broadcasted_iota(jnp.int32, (tokens, total), 1)
    expert = (((slot // share) * NLO + lo) * 2 + (slot // (4 * slots)) % 2).astype(F32)
    rank_of = (slot % slots).astype(F32)
    group_of = (slot // slots) % 4
    token = lax.broadcasted_iota(jnp.int32, (tokens, total), 0)
    lower = (
        lax.broadcasted_iota(jnp.int32, (tokens, tokens), 0)
        >= lax.broadcasted_iota(jnp.int32, (tokens, tokens), 1)
    ).astype(F32).astype(BF)
    placed_parts, weighted = [], []
    for group in range(4):
        packed = rows[group][parts * tokens :, :tokens]
        named = lax.dot_general(eye(tokens), packed, NT_DIMS, preferred_element_type=F32)
        metas[group * tokens : (group + 1) * tokens] = named
        hit = jnp.zeros((tokens, total), F32)
        weight = jnp.zeros((tokens, total), F32)
        for k in range(8):
            same = named[:, k : k + 1] == expert
            hit += same.astype(F32)
            weight += jnp.where(same, named[:, 8 + k : 9 + k], 0.0)
        hit = jnp.where(group_of == group, hit, 0.0)
        rank = jnp.dot(lower, hit.astype(BF), preferred_element_type=F32)
        placed = jnp.where(rank == rank_of + 1.0, hit, 0.0)
        step = group + 1
        offset = jnp.where(core == 0, -step, step if group < 3 else 0)
        position = (y * NLO + (lo + offset + NLO) % NLO) * tokens + token
        placed_parts.append(placed)
        weighted.append(jnp.where(position < length, placed * weight, 0.0))
    matrix = jnp.concatenate(placed_parts, axis=0).T.astype(BF)
    weight_matrix = jnp.concatenate(weighted, axis=0).astype(BF)
    placing[...] = matrix
    ones = jnp.ones((4 * tokens, width), BF)
    coefs = lax.dot_general(weight_matrix, ones, TN_DIMS, preferred_element_type=F32) * scale[0]
    for blocks, start in ((rows, 0), (grads, parts * width)):
        for part in range(parts):
            here = jnp.concatenate([b[part * tokens : (part + 1) * tokens] for b in blocks], axis=0)
            chosen = jnp.dot(matrix, here, preferred_element_type=F32)
            if start:
                chosen = chosen * coefs
            chosen = chosen.astype(BF)
            at = start + part * width
            for step in range(NY):
                sends[step, :, at : at + width] = chosen[step * share : (step + 1) * share]


def of_expert(routes, expert, start, size):
    half = routes.shape[1] // 2
    here = slice(expert * half, (expert + 1) * half)
    return jnp.concatenate([routes[step, here, start : start + size] for step in range(NY)], axis=0)


def expert_kernel(where, routes, gate_up, down, gate_up_other, down_other, returns, acts, acts_other):
    half = routes.shape[1] // 2
    features = routes.shape[2] // 2
    y = where[0]
    units = down.shape[1]
    lane = lax.broadcasted_iota(jnp.int32, (half, META), 1)
    for expert in range(2):
        inputs = of_expert(routes, expert, 0, features).T
        cotangents = of_expert(routes, expert, features, features).T
        back = jnp.zeros((NY * half, features), F32)
        gate = jnp.zeros((1, NY * half), F32)
        for w_in, w_out, acts_here in ((gate_up, down, acts), (gate_up_other, down_other, acts_other)):
            w_gate, w_up = w_in[expert, 0], w_in[expert, 1]
            pre_gate = jnp.dot(w_gate, inputs, preferred_element_type=F32)
            pre_up = jnp.dot(w_up, inputs, preferred_element_type=F32)
            hidden_grad = jnp.dot(w_out[expert], cotangents, preferred_element_type=F32)
            sigmoid = jax.nn.sigmoid(pre_gate)
            active = pre_gate * sigmoid
            slope = sigmoid * (1.0 + pre_gate * (1.0 - sigmoid))
            hidden = (active * pre_up).astype(BF)
            gate += jnp.sum(hidden.astype(F32) * hidden_grad, axis=0, keepdims=True)
            act_gate = (hidden_grad * pre_up * slope).astype(BF)
            act_up = (hidden_grad * active).astype(BF)
            acts_here[expert, 0] = act_gate
            acts_here[expert, 1] = act_up
            acts_here[expert, 2] = hidden
            back += lax.dot_general(act_gate, w_gate, TN_DIMS, preferred_element_type=F32)
            back += lax.dot_general(act_up, w_up, TN_DIMS, preferred_element_type=F32)
        back = back.astype(BF)
        gate_rows = jnp.broadcast_to(gate, (META, NY * half)).astype(BF)
        gate_columns = lax.dot_general(eye(NY * half), gate_rows, NT_DIMS, preferred_element_type=F32)
        for step in range(NY):
            here = slice(expert * half, (expert + 1) * half)
            there = slice(step * half, (step + 1) * half)
            returns[step, here, :features] = back[there]
            returns[step, here, features:] = jnp.where(
                lane == y * 2 + expert, gate_columns[there], 0.0
            ).astype(BF)


def weight_grad_kernel(routes, routes_other, acts, acts_other, out):
    units = acts.shape[2]
    features = routes.shape[2] // 2

    def both(expert, start):
        pieces = [of_expert(r, expert, start, features) for r in (routes, routes_other)]
        return jnp.concatenate(pieces, axis=0)

    for expert in range(2):
        inputs = both(expert, 0)
        cotangents = both(expert, features)
        for which, right, at in (
            (0, inputs, expert * 2 * units),
            (1, inputs, (expert * 2 + 1) * units),
            (2, cotangents, (4 + expert) * units),
        ):
            left = jnp.concatenate([acts[expert, which], acts_other[expert, which]], axis=1)
            out[at : at + units] = jnp.dot(left, right, preferred_element_type=F32).astype(BF)


def combine_kernel(where, placing, metas, returned, *outs):
    lo, core = where[1], where[3]
    features = returned.shape[2] - META
    back = jnp.concatenate([returned[step] for step in range(NY)], axis=0)
    summed = lax.dot_general(placing[...], back, TN_DIMS, preferred_element_type=F32)
    named = metas[:, :8]
    gate = jnp.zeros(named.shape, F32)
    for step in range(NY):
        for j in range(2):
            expert = (step * NLO + lo) * 2 + j
            at = features + step * 2 + j
            gate += jnp.where(named == expert.astype(F32), summed[:, at : at + 1], 0.0)
    tokens = outs[0].shape[0]
    for out, up, other in zip(outs, (3, 2, 1, 0), (2, 1, 0, 3), strict=True):
        a, b = (slice(g * tokens, (g + 1) * tokens) for g in (up, other))
        out[:, :features] = jnp.where(core == 0, summed[a, :features], summed[b, :features]).astype(BF)
        out[:, features:] = jnp.zeros((tokens, META), BF)
        out[:, features : features + 8] = jnp.where(core == 0, gate[a], gate[b]).astype(BF)


def split_core_kernel(where, arrived, below, kept, keep, give):
    tokens, features = arrived.shape[0], arrived.shape[1] - META
    width = features // (NHI * NCORE)
    first = where[3] == 0
    last = jnp.where(first, below[...].astype(F32), kept[...].astype(F32))
    total = arrived[...].astype(F32) + last
    gate = lax.dot_general(total[:, features:].astype(BF), eye(tokens), TN_DIMS, preferred_element_type=F32)
    for hi in range(NHI):
        blocks = []
        for part in (hi * NCORE, hi * NCORE + 1):
            row = jnp.broadcast_to(gate[part : part + 1], (16, tokens))
            blocks.append((total[:, part * width : (part + 1) * width], row))
        (zero, zero_gate), (one, one_gate) = blocks
        for out, swap in ((keep, first), (give, jnp.logical_not(first))):
            out[hi, :tokens] = jnp.where(swap, zero, one).astype(BF)
            out[hi, tokens:] = jnp.zeros((16, width), BF)
            out[hi, tokens:, :tokens] = jnp.where(swap, zero_gate, one_gate).astype(BF)


def finish_kernel(where, weights, pieces, weight_grads, input_grad, gate_grad, gate_up, down):
    experts, units = down.shape[:2]
    for expert in range(experts):
        at = expert * 2 * units
        gate_up[expert, 0] = weight_grads[at : at + units]
        gate_up[expert, 1] = weight_grads[at + units : at + 2 * units]
        at = (experts * 2 + expert) * units
        down[expert] = weight_grads[at : at + units]
    column = where[2] * NCORE + where[3]
    tokens = input_grad.shape[0]
    total = pieces[0].astype(F32)
    for hi in range(1, NHI):
        total += pieces[hi].astype(F32)
    input_grad[...] = total[:tokens].astype(BF)
    route = lax.broadcasted_iota(jnp.int32, weights.shape, 0)
    under = jnp.sum(jnp.where(route == column, weights[...].astype(F32), 0.0), axis=0, keepdims=True)
    gate_grad[...] = total[tokens : tokens + 1, :tokens] / under


def local(
    hidden_states,
    expert_ids,
    gate_weights,
    completion_lengths,
    output_grad,
    gate_up_proj,
    down_proj,
):
    tokens, width = hidden_states.shape
    parts = NHI * NCORE
    features = width * parts
    units = gate_up_proj.shape[2]
    slots = tokens * expert_ids.shape[1] // (NY * NLO * 2)
    total = NY * 2 * 4 * slots
    share = total // NY
    expert_at, tensor_at = lax.axis_index("expert"), lax.axis_index("tensor")
    where = jnp.stack(
        [
            expert_at // NLO,
            expert_at % NLO,
            tensor_at // NCORE,
            tensor_at % NCORE,
            completion_lengths[0],
        ]
    ).astype(jnp.int32)
    scale = ((tokens * NY * NLO) / completion_lengths.astype(F32)).astype(F32)
    weights_across = gate_weights.T
    meta = jnp.concatenate([expert_ids.T.astype(F32).astype(BF), weights_across], axis=0)
    meta = jnp.pad(meta, ((0, 0), (0, width - tokens)))

    gathered = lax.all_gather(
        jnp.concatenate([hidden_states, output_grad], axis=1), "tensor", axis=0, tiled=True
    )
    gathered, gate_up_kept, down_kept = lax.optimization_barrier((gathered, gate_up_proj, down_proj))
    gate_up_other, down_other = to_other_core(gate_up_kept), to_other_core(down_kept)
    rows = jnp.concatenate([gathered[:, :width], meta], axis=0)
    grads = gathered[:, width:]

    def onward(block):
        return send(block, lambda core: (0, 1 if core == 0 else -1, 0))

    def onward_last(block):
        return send(block, lambda core: (0, 1, 0) if core == 0 else None)

    row_blocks, grad_blocks = [rows], [grads]
    for _ in range(3):
        row_blocks.append(onward(row_blocks[-1]))
        grad_blocks.append(onward(grad_blocks[-1]))
    row_blocks = row_blocks[1:] + [onward_last(row_blocks[-1])]
    grad_blocks = grad_blocks[1:] + [onward_last(grad_blocks[-1])]
    grad_blocks[0], gate_up_other, down_other = lax.optimization_barrier(
        (grad_blocks[0], gate_up_other, down_other)
    )
    sends, placing, metas = call(
        select_kernel,
        [
            struct((NY, share, 2 * features)),
            struct((total, 4 * tokens)),
            struct((4 * tokens, 16), F32),
        ],
        where, scale, *row_blocks, rows, *grad_blocks, grads,
        scalars=2, flops=4 * 4 * tokens * total * features,
    )
    routes = swap_y(sends)
    acts_shape = struct((2, 3, units, total // 2))
    returns, acts, acts_theirs = call(
        expert_kernel,
        [struct((NY, share, features + META)), acts_shape, acts_shape],
        where, routes, gate_up_proj, down_proj, gate_up_other, down_other,
        scalars=1, flops=2 * total * 2 * units * features * 5,
    )
    acts_other = to_other_core(acts_theirs)
    kept_routes, acts = lax.optimization_barrier((routes, acts))
    routes_other = to_other_core(kept_routes)
    returned = swap_y(returns)
    (weight_parts,) = call(
        weight_grad_kernel,
        [struct((6 * units, features))],
        routes, routes_other, acts, acts_other,
        flops=2 * 2 * total * units * features * 3,
    )
    returned, weight_parts = lax.optimization_barrier((returned, weight_parts))
    far, next_far, near, last = call(
        combine_kernel,
        [struct((tokens, features + META))] * 4,
        where, placing, metas, returned, scalars=1, flops=2 * 4 * tokens * total * features,
    )

    weight_parts, far, next_far = lax.optimization_barrier((weight_parts, far, next_far))
    weight_grads = lax.psum_scatter(weight_parts, "dp", scatter_dimension=1, tiled=True)

    def two_back(block):
        return send(block, lambda core: (0, -2 if core == 0 else 2, 0))

    def add(one, other):
        return (one.astype(F32) + other.astype(F32)).astype(BF)

    near = add(near, two_back(far))
    last = add(last, two_back(next_far))
    arrived = send(near, lambda core: (0, -2 if core == 0 else 1, 0))
    below = send(last, lambda core: (0, -1, 0) if core == 0 else None)
    keep, give = call(
        split_core_kernel,
        [struct((NHI, tokens + 16, width))] * 2,
        where, arrived, below, last, scalars=1,
    )
    pieces = swap_hi(add(keep, to_other_core(give)))
    part = weight_grads.shape[1]
    input_grad, gate_grad, gate_up_grad, down_grad = call(
        finish_kernel,
        [
            struct((tokens, width)),
            struct((1, tokens), F32),
            struct((2, 2, units, part)),
            struct((2, units, part)),
        ],
        where, weights_across, pieces, weight_grads,
        scalars=1,
    )
    return (input_grad, gate_grad.reshape(tokens, 1), gate_up_grad, down_grad)


def solution(mesh):
    placed = (
        P(("dp", "expert"), "tensor"),
        P(("dp", "expert"), None),
        P(("dp", "expert"), None),
        P("dp"),
        P(("dp", "expert"), "tensor"),
        P("expert", None, "tensor", None),
        P("expert", "tensor", None),
    )
    return jax.shard_map(
        local,
        mesh=mesh,
        in_specs=placed,
        out_specs=(
            P(("dp", "expert"), "tensor"),
            P(("dp", "expert"), "tensor"),
            P("expert", None, "tensor", "dp"),
            P("expert", "tensor", "dp"),
        ),
        check_vma=False,
    )
```

```python
import functools

import jax
import jax.numpy as jnp
from jax import lax
from jax.experimental import pallas as pl
from jax.experimental.pallas import tpu as pltpu
from jax.sharding import PartitionSpec as P

BF = jnp.bfloat16
F32 = jnp.float32
NY, NLO, NHI, NCORE = 4, 8, 4, 2
NZ = NLO * NHI
META = 128
NT_DIMS = (((1,), (1,)), ((), ()))
TN_DIMS = (((0,), (0,)), ((), ()))
PLANE = ("expert", "tensor")
VMEM = pl.BlockSpec(memory_space=pltpu.VMEM)
SMEM = pl.BlockSpec(memory_space=pltpu.SMEM)
LIMIT = 28 * 1024 * 1024


def place(y, z, core):
    return ((y * NLO + z % NLO) * NHI + z // NLO) * NCORE + core


def send(array, to):
    pairs = []
    for y in range(NY):
        for z in range(NZ):
            for core in range(NCORE):
                step = to(core)
                if step is None:
                    continue
                dy, dz, dcore = step
                there = place((y + dy) % NY, (z + dz) % NZ, (core + dcore) % NCORE)
                pairs.append((place(y, z, core), there))
    return lax.ppermute(array, PLANE, pairs)


def both_cores(array):
    pairs = [[hi * NCORE + core for core in range(NCORE)] for hi in range(NHI)]
    return lax.all_gather(array, "tensor", axis_index_groups=pairs)


def swap_y(array):
    groups = [[y * NLO + lo for y in range(NY)] for lo in range(NLO)]
    return lax.all_to_all(
        array, "expert", split_axis=0, concat_axis=0, tiled=True, axis_index_groups=groups
    )


def swap_hi(array):
    groups = [[hi * NCORE + core for hi in range(NHI)] for core in range(NCORE)]
    return lax.all_to_all(
        array, "tensor", split_axis=0, concat_axis=0, tiled=True, axis_index_groups=groups
    )


def to_other_core(array):
    return send(array, lambda core: (0, 0, 1))


def call(kernel, outs, *args, scalars=0, flops=0):
    moved = sum(a.size * a.dtype.itemsize for a in args)
    moved += sum(o.size * o.dtype.itemsize for o in outs)
    ins = [SMEM if i < scalars else VMEM for i in range(len(args))]
    return pl.pallas_call(
        kernel,
        out_shape=outs,
        in_specs=ins,
        out_specs=[VMEM] * len(outs),
        compiler_params=pltpu.CompilerParams(vmem_limit_bytes=LIMIT),
        cost_estimate=pl.CostEstimate(flops=flops, bytes_accessed=moved, transcendentals=0),
    )(*args)


def struct(shape, dtype=BF):
    return jax.ShapeDtypeStruct(shape, dtype)


def eye(size):
    row = lax.broadcasted_iota(jnp.int32, (size, size), 0)
    column = lax.broadcasted_iota(jnp.int32, (size, size), 1)
    return (row == column).astype(F32).astype(BF)


def placing_kernel(where, scale, first, second, third, fourth, own, placing, back_placing, coefs, metas):
    y, lo, core, length = where[0], where[1], where[3], where[4]
    parts = NHI * NCORE
    width = own.shape[1]
    tokens = placing.shape[1] // 4
    total = placing.shape[0]
    share = total // NY
    slots = share // 8
    packed = [r[parts * tokens :, :tokens].astype(F32) for r in (first, second, third)]
    last = (fourth[parts * tokens :, :tokens].astype(F32), own[parts * tokens :, :tokens].astype(F32))
    packed.append(jnp.where(core == 0, *last))
    slot = lax.broadcasted_iota(jnp.int32, (tokens, total), 1)
    expert = (((slot // share) * NLO + lo) * 2 + (slot // (4 * slots)) % 2).astype(F32)
    rank_of = (slot % slots).astype(F32)
    group_of = (slot // slots) % 4
    token = lax.broadcasted_iota(jnp.int32, (tokens, total), 0)
    lower = (
        lax.broadcasted_iota(jnp.int32, (tokens, tokens), 0)
        >= lax.broadcasted_iota(jnp.int32, (tokens, tokens), 1)
    ).astype(F32).astype(BF)
    named_parts, placed_parts, weighted = [], [], []
    for group in range(4):
        named = lax.dot_general(
            eye(tokens), packed[group].astype(BF), NT_DIMS, preferred_element_type=F32
        )
        hit = jnp.zeros((tokens, total), F32)
        weight = jnp.zeros((tokens, total), F32)
        for k in range(8):
            same = named[:, k : k + 1] == expert
            hit += same.astype(F32)
            weight += jnp.where(same, named[:, 8 + k : 9 + k], 0.0)
        hit = jnp.where(group_of == group, hit, 0.0)
        rank = jnp.dot(lower, hit.astype(BF), preferred_element_type=F32)
        placed = jnp.where(rank == rank_of + 1.0, hit, 0.0)
        step = group + 1
        offset = jnp.where(core == 0, -step, step if group < 3 else 0)
        position = (y * NLO + (lo + offset + NLO) % NLO) * tokens + token
        named_parts.append(named)
        placed_parts.append(placed)
        weighted.append(jnp.where(position < length, placed * weight, 0.0))
    placing[...] = jnp.concatenate(placed_parts, axis=0).T.astype(BF)
    for at, (up, other) in enumerate(zip((3, 2, 1, 0), (2, 1, 0, 3), strict=True)):
        here = slice(at * tokens, (at + 1) * tokens)
        back_placing[here] = jnp.where(core == 0, placed_parts[up], placed_parts[other]).astype(BF)
        metas[here] = jnp.where(core == 0, named_parts[up], named_parts[other])
    weight_matrix = jnp.concatenate(weighted, axis=0).astype(BF)
    ones = jnp.ones((4 * tokens, width), BF)
    coefs[...] = lax.dot_general(weight_matrix, ones, TN_DIMS, preferred_element_type=F32) * scale[0]


def select_kernel(where, placing, coefs, *refs):
    row_refs, grad_refs, sends = refs[:5], refs[5:10], refs[10]
    core = where[3]
    parts = NHI * NCORE
    tokens = grad_refs[0].shape[0] // parts
    width = grad_refs[0].shape[1]
    share = placing.shape[0] // NY
    matrix = placing[...]
    for received, start in ((row_refs, 0), (grad_refs, parts * width)):
        for part in range(parts):
            piece = slice(part * tokens, (part + 1) * tokens)
            last = jnp.where(core == 0, received[3][piece].astype(F32), received[4][piece].astype(F32))
            blocks = [r[piece] for r in received[:3]] + [last.astype(BF)]
            chosen = jnp.dot(matrix, jnp.concatenate(blocks, axis=0), preferred_element_type=F32)
            if start:
                chosen = chosen * coefs[...]
            chosen = chosen.astype(BF)
            at = start + part * width
            for step in range(NY):
                sends[step, :, at : at + width] = chosen[step * share : (step + 1) * share]


def of_expert(routes, expert, start, size):
    half = routes.shape[1] // 2
    here = slice(expert * half, (expert + 1) * half)
    return jnp.concatenate([routes[step, here, start : start + size] for step in range(NY)], axis=0)


def expert_kernel(where, routes, gate_up, down, returns, acts):
    half = routes.shape[1] // 2
    features = routes.shape[2] // 2
    y, core = where[0], where[3]
    units = down.shape[2]
    lane = lax.broadcasted_iota(jnp.int32, (half, META), 1)
    for expert in range(2):
        inputs = of_expert(routes, expert, 0, features).T
        cotangents = of_expert(routes, expert, features, features).T
        back = jnp.zeros((NY * half, features), F32)
        gate = jnp.zeros((1, NY * half), F32)
        for side in range(NCORE):
            other = (core + side) % NCORE
            w_both = gate_up[side, expert].reshape(2 * units, features)
            pre = jnp.dot(w_both, inputs, preferred_element_type=F32)
            pre_gate, pre_up = pre[:units], pre[units:]
            hidden_grad = jnp.dot(down[side, expert], cotangents, preferred_element_type=F32)
            sigmoid = jax.nn.sigmoid(pre_gate)
            active = pre_gate * sigmoid
            slope = sigmoid * (1.0 + pre_gate * (1.0 - sigmoid))
            hidden = (active * pre_up).astype(BF)
            gate += jnp.sum(hidden.astype(F32) * hidden_grad, axis=0, keepdims=True)
            act_gate = (hidden_grad * pre_up * slope).astype(BF)
            act_up = (hidden_grad * active).astype(BF)
            acts[other, expert, 0] = act_gate
            acts[other, expert, 1] = act_up
            acts[other, expert, 2] = hidden
            act_both = jnp.concatenate([act_gate, act_up], axis=0)
            back += lax.dot_general(act_both, w_both, TN_DIMS, preferred_element_type=F32)
        back = back.astype(BF)
        gate_rows = jnp.broadcast_to(gate, (META, NY * half)).astype(BF)
        gate_columns = lax.dot_general(eye(NY * half), gate_rows, NT_DIMS, preferred_element_type=F32)
        for step in range(NY):
            here = slice(expert * half, (expert + 1) * half)
            there = slice(step * half, (step + 1) * half)
            returns[step, here, :features] = back[there]
            returns[step, here, features:] = jnp.where(
                lane == y * 2 + expert, gate_columns[there], 0.0
            ).astype(BF)


def weight_grad_kernel(routes, routes_other, acts, acts_other, out):
    units = acts.shape[3]
    features = routes.shape[2] // 2

    def both(expert, start):
        pieces = [of_expert(r, expert, start, features) for r in (routes, routes_other)]
        return jnp.concatenate(pieces, axis=0)

    for expert in range(2):
        inputs = both(expert, 0)
        cotangents = both(expert, features)
        for which, right, at in (
            (0, inputs, expert * 2 * units),
            (1, inputs, (expert * 2 + 1) * units),
            (2, cotangents, (4 + expert) * units),
        ):
            left = jnp.concatenate([acts[0, expert, which], acts_other[expert, which]], axis=1)
            out[at : at + units] = jnp.dot(left, right, preferred_element_type=F32).astype(BF)


def combine_kernel(where, placing, metas, returned, *outs):
    lo = where[1]
    features = returned.shape[2] - META
    back = jnp.concatenate([returned[step] for step in range(NY)], axis=0)
    tokens = outs[0].shape[0]
    for group, out in enumerate(outs):
        here = slice(group * tokens, (group + 1) * tokens)
        summed = jnp.dot(placing[here], back, preferred_element_type=F32)
        named = metas[here, :8]
        gate = jnp.zeros(named.shape, F32)
        for step in range(NY):
            for j in range(2):
                expert = (step * NLO + lo) * 2 + j
                at = features + step * 2 + j
                gate += jnp.where(named == expert.astype(F32), summed[:, at : at + 1], 0.0)
        out[:, :features] = summed[:, :features].astype(BF)
        out[:, features:] = jnp.zeros((tokens, META), BF)
        out[:, features : features + 8] = gate.astype(BF)


def split_core_kernel(where, arrived, below, kept, keep, give):
    tokens, features = arrived.shape[0], arrived.shape[1] - META
    width = features // (NHI * NCORE)
    first = where[3] == 0
    last = jnp.where(first, below[...].astype(F32), kept[...].astype(F32))
    total = arrived[...].astype(F32) + last
    gate = lax.dot_general(total[:, features:].astype(BF), eye(tokens), TN_DIMS, preferred_element_type=F32)
    for hi in range(NHI):
        blocks = []
        for part in (hi * NCORE, hi * NCORE + 1):
            row = jnp.broadcast_to(gate[part : part + 1], (16, tokens))
            blocks.append((total[:, part * width : (part + 1) * width], row))
        (zero, zero_gate), (one, one_gate) = blocks
        for out, swap in ((keep, first), (give, jnp.logical_not(first))):
            out[hi, :tokens] = jnp.where(swap, zero, one).astype(BF)
            out[hi, tokens:] = jnp.zeros((16, width), BF)
            out[hi, tokens:, :tokens] = jnp.where(swap, zero_gate, one_gate).astype(BF)


def part_kernel(weight_grads, gate_up, down):
    experts, units = down.shape[:2]
    for expert in range(experts):
        at = expert * 2 * units
        gate_up[expert, 0] = weight_grads[at : at + units]
        gate_up[expert, 1] = weight_grads[at + units : at + 2 * units]
        at = (experts * 2 + expert) * units
        down[expert] = weight_grads[at : at + units]


def finish_kernel(where, weights, pieces, input_grad, gate_grad):
    column = where[2] * NCORE + where[3]
    tokens = input_grad.shape[0]
    total = pieces[0].astype(F32)
    for hi in range(1, NHI):
        total += pieces[hi].astype(F32)
    input_grad[...] = total[:tokens].astype(BF)
    route = lax.broadcasted_iota(jnp.int32, weights.shape, 0)
    under = jnp.sum(jnp.where(route == column, weights[...].astype(F32), 0.0), axis=0, keepdims=True)
    gate_grad[...] = total[tokens : tokens + 1, :tokens] / under


def local(
    hidden_states,
    expert_ids,
    gate_weights,
    completion_lengths,
    output_grad,
    gate_up_proj,
    down_proj,
):
    tokens, width = hidden_states.shape
    parts = NHI * NCORE
    features = width * parts
    units = gate_up_proj.shape[2]
    slots = tokens * expert_ids.shape[1] // (NY * NLO * 2)
    total = NY * 2 * 4 * slots
    share = total // NY
    expert_at, tensor_at = lax.axis_index("expert"), lax.axis_index("tensor")
    where = jnp.stack(
        [
            expert_at // NLO,
            expert_at % NLO,
            tensor_at // NCORE,
            tensor_at % NCORE,
            completion_lengths[0],
        ]
    ).astype(jnp.int32)
    scale = ((tokens * NY * NLO) / completion_lengths.astype(F32)).astype(F32)
    weights_across = gate_weights.T
    meta = jnp.concatenate([expert_ids.T.astype(F32).astype(BF), weights_across], axis=0)
    meta = jnp.pad(meta, ((0, 0), (0, width - tokens)))

    gathered = lax.all_gather(
        jnp.concatenate([hidden_states, output_grad], axis=1), "tensor", axis=0, tiled=True
    )
    rows = jnp.concatenate([gathered[:, :width], meta], axis=0)
    grads = gathered[:, width:]

    def onward(block):
        return send(block, lambda core: (0, 1 if core == 0 else -1, 0))

    def onward_last(block):
        return send(block, lambda core: (0, 1, 0) if core == 0 else None)

    row_blocks, grad_blocks = [onward(rows)], [onward(grads)]
    for move in (onward, onward, onward_last):
        row_blocks.append(move(row_blocks[-1]))
        grad_blocks.append(move(grad_blocks[-1]))
    gate_up_both, down_both = both_cores(gate_up_proj), both_cores(down_proj)
    placing, back_placing, coefs, metas = call(
        placing_kernel,
        [
            struct((total, 4 * tokens)),
            struct((4 * tokens, total)),
            struct((total, width), F32),
            struct((4 * tokens, 16), F32),
        ],
        where, scale, *row_blocks, rows, scalars=2, flops=2 * 4 * tokens * total * width,
    )
    (sends,) = call(
        select_kernel,
        [struct((NY, share, 2 * features))],
        where, placing, coefs, *row_blocks, rows, *grad_blocks, grads,
        scalars=1, flops=4 * 4 * tokens * total * features,
    )
    routes = swap_y(sends)
    returns, acts = call(
        expert_kernel,
        [struct((NY, share, features + META)), struct((NCORE, 2, 3, units, total // 2))],
        where, routes, gate_up_both, down_both,
        scalars=1, flops=2 * total * 2 * units * features * 5,
    )
    acts_other = to_other_core(acts[1])
    kept_routes, acts = lax.optimization_barrier((routes, acts))
    routes_other = to_other_core(kept_routes)
    returned = swap_y(returns)
    (weight_parts,) = call(
        weight_grad_kernel,
        [struct((6 * units, features))],
        routes, routes_other, acts, acts_other,
        flops=2 * 2 * total * units * features * 3,
    )
    returned, weight_parts = lax.optimization_barrier((returned, weight_parts))
    far, next_far, near, last = call(
        combine_kernel,
        [struct((tokens, features + META))] * 4,
        where, back_placing, metas, returned, scalars=1, flops=2 * 4 * tokens * total * features,
    )

    weight_parts, far, next_far = lax.optimization_barrier((weight_parts, far, next_far))
    weight_grads = lax.psum_scatter(weight_parts, "dp", scatter_dimension=1, tiled=True)

    def two_back(block):
        return send(block, lambda core: (0, -2 if core == 0 else 2, 0))

    def add(one, other):
        return (one.astype(F32) + other.astype(F32)).astype(BF)

    near = add(near, two_back(far))
    last = add(last, two_back(next_far))
    arrived = send(near, lambda core: (0, -2 if core == 0 else 1, 0))
    below = send(last, lambda core: (0, -1, 0) if core == 0 else None)
    keep, give = call(
        split_core_kernel,
        [struct((NHI, tokens + 16, width))] * 2,
        where, arrived, below, last, scalars=1,
    )
    pieces = swap_hi(add(keep, to_other_core(give)))
    part = weight_grads.shape[1]
    gate_up_grad, down_grad = call(
        part_kernel, [struct((2, 2, units, part)), struct((2, units, part))], weight_grads
    )
    pieces, gate_up_grad, down_grad = lax.optimization_barrier((pieces, gate_up_grad, down_grad))
    input_grad, gate_grad = call(
        finish_kernel,
        [struct((tokens, width)), struct((1, tokens), F32)],
        where, weights_across, pieces, scalars=1,
    )
    return (input_grad, gate_grad.reshape(tokens, 1), gate_up_grad, down_grad)


def solution(mesh):
    placed = (
        P(("dp", "expert"), "tensor"),
        P(("dp", "expert"), None),
        P(("dp", "expert"), None),
        P("dp"),
        P(("dp", "expert"), "tensor"),
        P("expert", None, "tensor", None),
        P("expert", "tensor", None),
    )
    return jax.shard_map(
        local,
        mesh=mesh,
        in_specs=placed,
        out_specs=(
            P(("dp", "expert"), "tensor"),
            P(("dp", "expert"), "tensor"),
            P("expert", None, "tensor", "dp"),
            P("expert", "tensor", "dp"),
        ),
        check_vma=False,
    )
```

```python
import functools

import jax
import jax.numpy as jnp
from jax import lax
from jax.experimental import pallas as pl
from jax.experimental.pallas import tpu as pltpu
from jax.sharding import PartitionSpec as P

BF = jnp.bfloat16
F32 = jnp.float32
NY, NLO, NHI, NCORE = 4, 8, 4, 2
NZ = NLO * NHI
META = 128
NT_DIMS = (((1,), (1,)), ((), ()))
TN_DIMS = (((0,), (0,)), ((), ()))
PLANE = ("expert", "tensor")
VMEM = pl.BlockSpec(memory_space=pltpu.VMEM)
SMEM = pl.BlockSpec(memory_space=pltpu.SMEM)
LIMIT = 28 * 1024 * 1024


def place(y, z, core):
    return ((y * NLO + z % NLO) * NHI + z // NLO) * NCORE + core


def send(array, to):
    pairs = []
    for y in range(NY):
        for z in range(NZ):
            for core in range(NCORE):
                step = to(core)
                if step is None:
                    continue
                dy, dz, dcore = step
                there = place((y + dy) % NY, (z + dz) % NZ, (core + dcore) % NCORE)
                pairs.append((place(y, z, core), there))
    return lax.ppermute(array, PLANE, pairs)


def both_cores(array):
    pairs = [[hi * NCORE + core for core in range(NCORE)] for hi in range(NHI)]
    return lax.all_gather(array, "tensor", axis_index_groups=pairs)


def swap_y(array):
    groups = [[y * NLO + lo for y in range(NY)] for lo in range(NLO)]
    return lax.all_to_all(
        array, "expert", split_axis=0, concat_axis=0, tiled=True, axis_index_groups=groups
    )


def swap_hi(array):
    groups = [[hi * NCORE + core for hi in range(NHI)] for core in range(NCORE)]
    return lax.all_to_all(
        array, "tensor", split_axis=0, concat_axis=0, tiled=True, axis_index_groups=groups
    )


def to_other_core(array):
    return send(array, lambda core: (0, 0, 1))


def call(kernel, outs, *args, scalars=0, flops=0):
    moved = sum(a.size * a.dtype.itemsize for a in args)
    moved += sum(o.size * o.dtype.itemsize for o in outs)
    ins = [SMEM if i < scalars else VMEM for i in range(len(args))]
    return pl.pallas_call(
        kernel,
        out_shape=outs,
        in_specs=ins,
        out_specs=[VMEM] * len(outs),
        compiler_params=pltpu.CompilerParams(vmem_limit_bytes=LIMIT),
        cost_estimate=pl.CostEstimate(flops=flops, bytes_accessed=moved, transcendentals=0),
    )(*args)


def struct(shape, dtype=BF):
    return jax.ShapeDtypeStruct(shape, dtype)


def eye(size):
    row = lax.broadcasted_iota(jnp.int32, (size, size), 0)
    column = lax.broadcasted_iota(jnp.int32, (size, size), 1)
    return (row == column).astype(F32).astype(BF)


def placing_kernel(where, scale, first, second, third, fourth, own, placing, back_placing, coefs, metas):
    y, lo, core, length = where[0], where[1], where[3], where[4]
    parts = NHI * NCORE
    width = own.shape[1]
    tokens = placing.shape[1] // 4
    total = placing.shape[0]
    share = total // NY
    slots = share // 8
    packed = [r[parts * tokens :, :tokens].astype(F32) for r in (first, second, third)]
    last = (fourth[parts * tokens :, :tokens].astype(F32), own[parts * tokens :, :tokens].astype(F32))
    packed.append(jnp.where(core == 0, *last))
    slot = lax.broadcasted_iota(jnp.int32, (tokens, total), 1)
    expert = (((slot // share) * NLO + lo) * 2 + (slot // (4 * slots)) % 2).astype(F32)
    rank_of = (slot % slots).astype(F32)
    group_of = (slot // slots) % 4
    token = lax.broadcasted_iota(jnp.int32, (tokens, total), 0)
    lower = (
        lax.broadcasted_iota(jnp.int32, (tokens, tokens), 0)
        >= lax.broadcasted_iota(jnp.int32, (tokens, tokens), 1)
    ).astype(F32).astype(BF)
    named_parts, placed_parts, weighted = [], [], []
    for group in range(4):
        named = lax.dot_general(
            eye(tokens), packed[group].astype(BF), NT_DIMS, preferred_element_type=F32
        )
        hit = jnp.zeros((tokens, total), F32)
        weight = jnp.zeros((tokens, total), F32)
        for k in range(8):
            same = named[:, k : k + 1] == expert
            hit += same.astype(F32)
            weight += jnp.where(same, named[:, 8 + k : 9 + k], 0.0)
        hit = jnp.where(group_of == group, hit, 0.0)
        rank = jnp.dot(lower, hit.astype(BF), preferred_element_type=F32)
        placed = jnp.where(rank == rank_of + 1.0, hit, 0.0)
        step = group + 1
        offset = jnp.where(core == 0, -step, step if group < 3 else 0)
        position = (y * NLO + (lo + offset + NLO) % NLO) * tokens + token
        named_parts.append(named)
        placed_parts.append(placed)
        weighted.append(jnp.where(position < length, placed * weight, 0.0))
    placing[...] = jnp.concatenate(placed_parts, axis=0).T.astype(BF)
    for at, (up, other) in enumerate(zip((3, 2, 1, 0), (2, 1, 0, 3), strict=True)):
        here = slice(at * tokens, (at + 1) * tokens)
        back_placing[here] = jnp.where(core == 0, placed_parts[up], placed_parts[other]).astype(BF)
        metas[here] = jnp.where(core == 0, named_parts[up], named_parts[other])
    weight_matrix = jnp.concatenate(weighted, axis=0).astype(BF)
    ones = jnp.ones((4 * tokens, width), BF)
    coefs[...] = lax.dot_general(weight_matrix, ones, TN_DIMS, preferred_element_type=F32) * scale[0]


def select_kernel(where, placing, coefs, *refs):
    row_refs, grad_refs, sends = refs[:5], refs[5:10], refs[10]
    core = where[3]
    parts = NHI * NCORE
    tokens = grad_refs[0].shape[0] // parts
    width = grad_refs[0].shape[1]
    share = placing.shape[0] // NY
    matrix = placing[...]
    for received, start in ((row_refs, 0), (grad_refs, parts * width)):
        for part in range(parts):
            piece = slice(part * tokens, (part + 1) * tokens)
            last = jnp.where(core == 0, received[3][piece].astype(F32), received[4][piece].astype(F32))
            blocks = [r[piece] for r in received[:3]] + [last.astype(BF)]
            chosen = jnp.dot(matrix, jnp.concatenate(blocks, axis=0), preferred_element_type=F32)
            if start:
                chosen = chosen * coefs[...]
            chosen = chosen.astype(BF)
            at = start + part * width
            for step in range(NY):
                sends[step, :, at : at + width] = chosen[step * share : (step + 1) * share]


def of_expert(routes, expert, start, size):
    half = routes.shape[1] // 2
    here = slice(expert * half, (expert + 1) * half)
    return jnp.concatenate([routes[step, here, start : start + size] for step in range(NY)], axis=0)


def expert_kernel(where, routes, gate_up, down, returns, acts):
    half = routes.shape[1] // 2
    features = routes.shape[2] // 2
    y, core = where[0], where[3]
    units = down.shape[2]
    lane = lax.broadcasted_iota(jnp.int32, (half, META), 1)
    for expert in range(2):
        inputs = of_expert(routes, expert, 0, features).T
        cotangents = of_expert(routes, expert, features, features).T
        back = jnp.zeros((NY * half, features), F32)
        gate = jnp.zeros((1, NY * half), F32)
        for side in range(NCORE):
            other = (core + side) % NCORE
            w_both = gate_up[side, expert].reshape(2 * units, features)
            pre = jnp.dot(w_both, inputs, preferred_element_type=F32)
            pre_gate, pre_up = pre[:units], pre[units:]
            hidden_grad = jnp.dot(down[side, expert], cotangents, preferred_element_type=F32)
            sigmoid = jax.nn.sigmoid(pre_gate)
            active = pre_gate * sigmoid
            slope = sigmoid * (1.0 + pre_gate * (1.0 - sigmoid))
            hidden = (active * pre_up).astype(BF)
            gate += jnp.sum(hidden.astype(F32) * hidden_grad, axis=0, keepdims=True)
            act_gate = (hidden_grad * pre_up * slope).astype(BF)
            act_up = (hidden_grad * active).astype(BF)
            acts[other, expert, 0] = act_gate
            acts[other, expert, 1] = act_up
            acts[other, expert, 2] = hidden
            act_both = jnp.concatenate([act_gate, act_up], axis=0)
            back += lax.dot_general(act_both, w_both, TN_DIMS, preferred_element_type=F32)
        back = back.astype(BF)
        gate_rows = jnp.broadcast_to(gate, (META, NY * half)).astype(BF)
        gate_columns = lax.dot_general(eye(NY * half), gate_rows, NT_DIMS, preferred_element_type=F32)
        for step in range(NY):
            here = slice(expert * half, (expert + 1) * half)
            there = slice(step * half, (step + 1) * half)
            returns[step, here, :features] = back[there]
            returns[step, here, features:] = jnp.where(
                lane == y * 2 + expert, gate_columns[there], 0.0
            ).astype(BF)


def weight_grad_kernel(routes, routes_other, acts, acts_other, out):
    units = acts.shape[3]
    features = routes.shape[2] // 2

    def both(expert, start):
        pieces = [of_expert(r, expert, start, features) for r in (routes, routes_other)]
        return jnp.concatenate(pieces, axis=0)

    for expert in range(2):
        inputs = both(expert, 0)
        cotangents = both(expert, features)
        for which, right, at in (
            (0, inputs, expert * 2 * units),
            (1, inputs, (expert * 2 + 1) * units),
            (2, cotangents, (4 + expert) * units),
        ):
            left = jnp.concatenate([acts[0, expert, which], acts_other[expert, which]], axis=1)
            out[at : at + units] = jnp.dot(left, right, preferred_element_type=F32).astype(BF)


def combine_kernel(where, placing, metas, returned, *outs):
    lo = where[1]
    features = returned.shape[2] - META
    back = jnp.concatenate([returned[step] for step in range(NY)], axis=0)
    tokens = outs[0].shape[0]
    for group, out in enumerate(outs):
        here = slice(group * tokens, (group + 1) * tokens)
        summed = jnp.dot(placing[here], back, preferred_element_type=F32)
        named = metas[here, :8]
        gate = jnp.zeros(named.shape, F32)
        for step in range(NY):
            for j in range(2):
                expert = (step * NLO + lo) * 2 + j
                at = features + step * 2 + j
                gate += jnp.where(named == expert.astype(F32), summed[:, at : at + 1], 0.0)
        out[:, :features] = summed[:, :features].astype(BF)
        out[:, features:] = jnp.zeros((tokens, META), BF)
        out[:, features : features + 8] = gate.astype(BF)


def split_core_kernel(where, arrived, below, kept, keep, give):
    tokens, features = arrived.shape[0], arrived.shape[1] - META
    width = features // (NHI * NCORE)
    first = where[3] == 0
    last = jnp.where(first, below[...].astype(F32), kept[...].astype(F32))
    total = arrived[...].astype(F32) + last
    gate = lax.dot_general(total[:, features:].astype(BF), eye(tokens), TN_DIMS, preferred_element_type=F32)
    for hi in range(NHI):
        blocks = []
        for part in (hi * NCORE, hi * NCORE + 1):
            row = jnp.broadcast_to(gate[part : part + 1], (16, tokens))
            blocks.append((total[:, part * width : (part + 1) * width], row))
        (zero, zero_gate), (one, one_gate) = blocks
        for out, swap in ((keep, first), (give, jnp.logical_not(first))):
            out[hi, :tokens] = jnp.where(swap, zero, one).astype(BF)
            out[hi, tokens:] = jnp.zeros((16, width), BF)
            out[hi, tokens:, :tokens] = jnp.where(swap, zero_gate, one_gate).astype(BF)


def part_kernel(weight_grads, gate_up, down):
    experts, units = down.shape[:2]
    for expert in range(experts):
        at = expert * 2 * units
        gate_up[expert, 0] = weight_grads[at : at + units]
        gate_up[expert, 1] = weight_grads[at + units : at + 2 * units]
        at = (experts * 2 + expert) * units
        down[expert] = weight_grads[at : at + units]


def finish_kernel(where, weights, pieces, input_grad, gate_grad):
    column = where[2] * NCORE + where[3]
    tokens = input_grad.shape[0]
    total = pieces[0].astype(F32)
    for hi in range(1, NHI):
        total += pieces[hi].astype(F32)
    input_grad[...] = total[:tokens].astype(BF)
    route = lax.broadcasted_iota(jnp.int32, weights.shape, 0)
    under = jnp.sum(jnp.where(route == column, weights[...].astype(F32), 0.0), axis=0, keepdims=True)
    gate_grad[...] = total[tokens : tokens + 1, :tokens] / under


def local(
    hidden_states,
    expert_ids,
    gate_weights,
    completion_lengths,
    output_grad,
    gate_up_proj,
    down_proj,
):
    tokens, width = hidden_states.shape
    parts = NHI * NCORE
    features = width * parts
    units = gate_up_proj.shape[2]
    slots = tokens * expert_ids.shape[1] // (NY * NLO * 2)
    total = NY * 2 * 4 * slots
    share = total // NY
    expert_at, tensor_at = lax.axis_index("expert"), lax.axis_index("tensor")
    where = jnp.stack(
        [
            expert_at // NLO,
            expert_at % NLO,
            tensor_at // NCORE,
            tensor_at % NCORE,
            completion_lengths[0],
        ]
    ).astype(jnp.int32)
    scale = ((tokens * NY * NLO) / completion_lengths.astype(F32)).astype(F32)
    weights_across = gate_weights.T
    meta = jnp.concatenate([expert_ids.T.astype(F32).astype(BF), weights_across], axis=0)
    meta = jnp.pad(meta, ((0, 0), (0, width - tokens)))

    gathered = lax.all_gather(
        jnp.concatenate([hidden_states, output_grad], axis=1), "tensor", axis=0, tiled=True
    )
    rows = jnp.concatenate([gathered[:, :width], meta], axis=0)
    grads = gathered[:, width:]

    def onward(block):
        return send(block, lambda core: (0, 1 if core == 0 else -1, 0))

    def onward_last(block):
        return send(block, lambda core: (0, 1, 0) if core == 0 else None)

    row_blocks, grad_blocks = [onward(rows)], [onward(grads)]
    for move in (onward, onward, onward_last):
        row_blocks.append(move(row_blocks[-1]))
        grad_blocks.append(move(grad_blocks[-1]))
    gate_up_both, down_both = both_cores(gate_up_proj), both_cores(down_proj)
    placing, back_placing, coefs, metas = call(
        placing_kernel,
        [
            struct((total, 4 * tokens)),
            struct((4 * tokens, total)),
            struct((total, width), F32),
            struct((4 * tokens, 16), F32),
        ],
        where, scale, *row_blocks, rows, scalars=2, flops=2 * 4 * tokens * total * width,
    )
    (sends,) = call(
        select_kernel,
        [struct((NY, share, 2 * features))],
        where, placing, coefs, *row_blocks, rows, *grad_blocks, grads,
        scalars=1, flops=4 * 4 * tokens * total * features,
    )
    sends, gate_up_both, down_both = lax.optimization_barrier((sends, gate_up_both, down_both))
    routes = swap_y(sends)
    returns, acts = call(
        expert_kernel,
        [struct((NY, share, features + META)), struct((NCORE, 2, 3, units, total // 2))],
        where, routes, gate_up_both, down_both,
        scalars=1, flops=2 * total * 2 * units * features * 5,
    )
    kept_routes, returned = lax.optimization_barrier((routes, swap_y(returns)))
    acts_other, routes_other = to_other_core(acts[1]), to_other_core(kept_routes)
    (weight_parts,) = call(
        weight_grad_kernel,
        [struct((6 * units, features))],
        routes, routes_other, acts, acts_other,
        flops=2 * 2 * total * units * features * 3,
    )
    far, next_far, near, last = call(
        combine_kernel,
        [struct((tokens, features + META))] * 4,
        where, back_placing, metas, returned, scalars=1, flops=2 * 4 * tokens * total * features,
    )

    def two_back(block):
        return send(block, lambda core: (0, -2 if core == 0 else 2, 0))

    def add(one, other):
        return (one.astype(F32) + other.astype(F32)).astype(BF)

    weight_parts, far, next_far = lax.optimization_barrier(
        (weight_parts, two_back(far), two_back(next_far))
    )
    weight_grads = lax.psum_scatter(weight_parts, "dp", scatter_dimension=1, tiled=True)
    near = add(near, far)
    last = add(last, next_far)
    arrived = send(near, lambda core: (0, -2 if core == 0 else 1, 0))
    below = send(last, lambda core: (0, -1, 0) if core == 0 else None)
    keep, give = call(
        split_core_kernel,
        [struct((NHI, tokens + 16, width))] * 2,
        where, arrived, below, last, scalars=1,
    )
    pieces = swap_hi(add(keep, to_other_core(give)))
    part = weight_grads.shape[1]
    gate_up_grad, down_grad = call(
        part_kernel, [struct((2, 2, units, part)), struct((2, units, part))], weight_grads
    )
    pieces, gate_up_grad, down_grad = lax.optimization_barrier((pieces, gate_up_grad, down_grad))
    input_grad, gate_grad = call(
        finish_kernel,
        [struct((tokens, width)), struct((1, tokens), F32)],
        where, weights_across, pieces, scalars=1,
    )
    return (input_grad, gate_grad.reshape(tokens, 1), gate_up_grad, down_grad)


def solution(mesh):
    placed = (
        P(("dp", "expert"), "tensor"),
        P(("dp", "expert"), None),
        P(("dp", "expert"), None),
        P("dp"),
        P(("dp", "expert"), "tensor"),
        P("expert", None, "tensor", None),
        P("expert", "tensor", None),
    )
    return jax.shard_map(
        local,
        mesh=mesh,
        in_specs=placed,
        out_specs=(
            P(("dp", "expert"), "tensor"),
            P(("dp", "expert"), "tensor"),
            P("expert", None, "tensor", "dp"),
            P("expert", "tensor", "dp"),
        ),
        check_vma=False,
    )
```
